32 devices in a mesh: groups: 2 (over y), gy: 16 (over z, x, core).
Axes of the slice: x: 2, y: 2, z: 4, core: 2. Of those that a mesh axis runs over, the one named last changes fastest.
Arguments:
- adjoint: float32 [16, 256, 1024], P('groups', 'gy'), parts along dimension 0, may hold values from -6 to 6
- coeffs: float32 [4, 256, 1024], P(None, 'gy'), may hold values from 0.1 to 0.24
- dist: int32 [256, 1024], P('gy'), may hold values from 0 to 16, as said below
- sources: int32 [2048, 128], P('gy'), may hold values from 0 to 16383, as said below
- weights: bfloat16 [2048, 128, 128], P('gy'), may hold values from -0.5 to 0.5
- owners: int32 [2048, 1], P('gy'), may hold values from 0 to 15; in each aligned block of 128 rows (0 to 127, 128 to 255, ...) at most 16 rows name the same one
- slots: int32 [2048], P('gy'), may hold values from 0 to 31
- counts: int32 [16], P('gy'), may hold values from 96 to 128, as said below
Outputs:
- grad_state: float32 [16, 256, 1024], P('groups', 'gy'), parts along dimension 0
- host_adjoint: float32 [512, 16, 128], P('gy', 'groups'), parts along dimension 1
The draws below stay inside these ranges and needn't reach their ends.
There are 2 independent parts, one for each index of `groups`. The reference program is written for one: setup_inputs(seed, part) draws one part's arguments, and reference() takes and returns one part's arrays. A program takes and returns all parts, laid end to end along the dimension named above; an argument that names none is the same for every part. Nothing has to cross between parts.
Inputs may be any that keep to these rules, and one draw needn't show every extreme that they name: `owners`: within the 128 blocks of one device at most 16 name one owner, a bound that some block reaches. `counts`: a device's blocks b with b < its count are live, the rest padding; the first and last device have 128 live blocks. `sources`: each entry is row * 1024 + column of a cell of the device's own rows, within 16 columns of the left or right edge. `dist`: a cell's distance to the grid's edge plus 0 to 2, capped at 16.
All inputs are finite; a program needn't handle non-finite values.
Results may differ from the reference program's by a relative error of at most 0.0029.
Values sent between devices are 32-bit elements; how exact they have to be, the bound alone decides.
A program may use at most 64 MiB of HBM per device.

```python
import math
import jax
import jax.numpy as jnp
import numpy as np
from jax import lax

LEV = 8
ROWS = 16
NX = 1024
ZW = 16
SUB = 4
BS = 128
HB = 128
NBLK = 128
HOST_BLK = 32
CAP = 16
NY = 256
NB = 2048
N_GY = 16


def draw_dist(key, part):
    key = jax.random.fold_in(key, 11)
    row_pos = lax.broadcasted_iota(jnp.int32, (NY, NX), 0)
    col_pos = lax.broadcasted_iota(jnp.int32, (NY, NX), 1)
    edge = jnp.minimum(jnp.minimum(row_pos, NY - 1 - row_pos), jnp.minimum(col_pos, NX - 1 - col_pos))
    jitter = jax.random.randint(key, (NY, NX), 0, 3)
    return jnp.minimum(edge + jitter, ZW).astype(jnp.int32)


def draw_sources(key, part):
    key = jax.random.fold_in(key, 23)
    key_row, key_side, key_depth = jax.random.split(key, 3)
    shape = (NB, BS)
    row_pick = jax.random.randint(key_row, shape, 0, ROWS)
    side_pick = jax.random.randint(key_side, shape, 0, 2)
    depth = jax.random.randint(key_depth, shape, 0, ZW)
    column = jnp.where(side_pick == 0, depth, NX - 1 - depth)
    return (row_pick * NX + column).astype(jnp.int32)


def draw_counts(key, part):
    key = jax.random.fold_in(key, 37)
    place = lax.iota(jnp.int32, N_GY)
    inner = jax.random.randint(key, (N_GY,), max(1, 3 * NBLK // 4), NBLK + 1)
    return jnp.where((place == 0) | (place == N_GY - 1), NBLK, inner).astype(jnp.int32)


def plant(drawn, rng, least, top_value):
    longest = drawn.shape.index(max(drawn.shape))
    spots = []
    for shift in (0, 1):
        where = [jax.random.randint(jax.random.fold_in(rng, axis), (), 0, length) for axis, length in enumerate(drawn.shape)]
        where[longest] = (where[longest] + shift) % drawn.shape[longest]
        spots.append(tuple(where))
    return drawn.at[spots[0]].set(least).at[spots[1]].set(top_value)


def steps_of(stream_key, extent, shards, low, high):
    def one(axis_at, shards_of):
        draws = jax.random.uniform(jax.random.fold_in(jax.random.fold_in(stream_key, 6), axis_at), (shards_of,), jnp.float32, low / len(shards), high / len(shards))
        return jnp.repeat(jnp.exp(draws), extent[axis_at] // shards_of).reshape((-1,) + (1,) * (len(extent) - axis_at - 1))

    factor_of = one(*shards[0])
    for cut in shards[1:]:
        factor_of = factor_of * one(*cut)
    return factor_of


def assign_block(key, own, number, rows, amount, top, bound, skew):
    order = jax.random.permutation(key, amount)
    packed, common = load_shares(amount, rows * top, bound, skew, True), load_shares(amount, rows * top, bound, skew, False)
    places = jnp.arange(amount)

    def named(sizes, offset_by):
        used = int((sizes > 0).sum())
        fixed = max(1, used // 4)
        moved = fixed + (places - fixed + offset_by * (used - fixed)) % max(1, amount - fixed)
        return jnp.zeros((amount,), jnp.int32).at[order[jnp.where(places < fixed, places, moved)]].set(jnp.asarray(sizes, jnp.int32))

    sizes = jnp.where(number % 4 == 0, named(packed, number // 4), named(common, number - number // 4 - 1))
    mixed = jax.random.permutation(jax.random.fold_in(own, 3), amount)
    source_of, taker = mixed[0:amount // 2 * 2:2], mixed[1:amount // 2 * 2:2]
    margin = jnp.minimum(sizes[source_of] - 1, bound - sizes[taker]) // 2
    margin = jnp.where((source_of == order[0]) | (taker == order[0]) | (sizes[taker] == 0), 0, jnp.maximum(margin, 0))
    moved = jax.random.randint(jax.random.fold_in(own, 4), (amount // 2,), 0, 1 << 20) % (margin + 1)
    sizes = sizes.at[source_of].add(-moved).at[taker].add(moved)
    items = jnp.searchsorted(jnp.cumsum(sizes), jnp.arange(rows * top), side="right").astype(jnp.int32)
    grid = items.reshape(top, rows).T
    grid = grid[jax.random.permutation(jax.random.fold_in(own, 1), rows)]
    offset_by = jax.random.randint(jax.random.fold_in(own, 2), (rows, 1), 0, top)
    return jnp.take_along_axis(grid, (jnp.arange(top)[None, :] + offset_by) % top, axis=1)


def load_shares(count, total, reach, slope, full):
    weights = [(1 << 20) // math.isqrt(grade ** slope) + 1 for grade in range(1, count + 1)]
    largest = reach if full else min(reach, max(-(-total // count), total * weights[0] // sum(weights)))
    least = 1 if total - largest >= count - 1 else 0
    holding, surplus = [largest] + [least] * (count - 1), total - largest - least * (count - 1)
    while surplus > 0:
        free = [i for i in range(1, count) if holding[i] < largest] or [i for i in range(1, count) if holding[i] < reach]
        mass, remaining = sum([weights[i] for i in free]), surplus
        for i in free:
            more = min(reach - holding[i], max(1, remaining * weights[i] // mass), surplus)
            holding[i] = holding[i] + more
            surplus = surplus - more
    return np.array(holding)


def noise(rng, dims, deviation, limit, shards=(), held_as=jnp.bfloat16):
    level = steps_of(rng, dims, shards, -0.22, 0.18) if shards else 1.0
    entries = jax.random.normal(rng, dims, jnp.float32) * deviation * level
    return jnp.minimum(jnp.maximum(entries, -limit), limit).astype(held_as)


def setup_inputs(seed: int = 0, part: int = 0) -> dict:
    splits = jax.random.split(jax.random.key(seed), 9)
    part_splits = jax.random.split(jax.random.fold_in(splits[8], part), 9)
    adjoint = noise(part_splits[0], (LEV, NY, NX), 1.0, 6.0, ((1, 16),), jnp.float32)
    coeffs = jnp.clip(0.1 + 0.13999999 * jax.random.uniform(splits[1], (4, NY, NX), jnp.float32) ** steps_of(splits[1], (4, NY, NX), ((1, 16),), -0.2, 0.2), 0.1, 0.24)
    dist = draw_dist(jax.random.fold_in(splits[8], 71), part)
    sources = draw_sources(jax.random.fold_in(splits[8], 71), part)
    weights = noise(splits[4], (NB, BS, HB), BS ** -0.5, 0.5, ((0, 16),))
    owners_keys = jax.random.split(jax.random.fold_in(splits[5], 1), NB // NBLK)
    owners_turns = jax.random.permutation(jax.random.fold_in(splits[5], 3), NB // NBLK)
    owners = jax.vmap(lambda own, number: assign_block(jax.random.fold_in(splits[5], 2), own, number, NBLK, N_GY, 1, CAP, 1))(owners_keys, owners_turns).reshape((NB, 1))
    slots = plant(jax.random.randint(splits[6], (NB,), 0, HOST_BLK), jax.random.fold_in(splits[6], 1), 0, HOST_BLK - 1).astype(jnp.int32)
    counts = draw_counts(jax.random.fold_in(splits[8], 71), part)
    return {"adjoint": adjoint, "coeffs": coeffs, "dist": dist, "sources": sources, "weights": weights, "owners": owners, "slots": slots, "counts": counts}


def davies(dist):
    frac = 1.0 - dist.astype(jnp.float32) / ZW
    return frac * frac


def sweep(field, coeffs):
    k_north, k_south, k_west, k_east = coeffs[0], coeffs[1], coeffs[2], coeffs[3]
    total = k_north + k_south + k_west + k_east
    g_north = k_north * field
    g_south = k_south * field
    g_west = k_west * field
    g_east = k_east * field
    zero_row = jnp.zeros_like(field[:, :1, :])
    zero_col = jnp.zeros_like(field[:, :, :1])
    upper = jnp.concatenate([g_north[:, 1:, :], zero_row], 1)
    lower = jnp.concatenate([zero_row, g_south[:, :-1, :]], 1)
    left_part = jnp.concatenate([g_west[:, :, 1:], zero_col], 2)
    right_part = jnp.concatenate([zero_col, g_east[:, :, :-1]], 2)
    return field * (1.0 - total) + upper + lower + left_part + right_part


def reference(adjoint, coeffs, dist, sources, weights, owners, slots, counts):
    relax = davies(dist)
    field = (1.0 - relax) * adjoint
    for step in range(SUB):
        field = sweep(field, coeffs)
    zone_flat = (relax * adjoint).reshape(LEV, N_GY, ROWS * NX)
    src = sources.reshape(N_GY, NBLK, BS)
    wts = weights.reshape(N_GY, NBLK, BS, HB)
    live = jnp.arange(NBLK).astype(jnp.int32)[None, :] < counts[:, None]

    def one_device(items):
        zone_dev, src_dev, wts_dev, live_dev = items
        values = jnp.take(zone_dev, src_dev, axis=1).astype(jnp.bfloat16)
        prod = jnp.einsum("lbk,bkh->blh", values.astype(jnp.float32), wts_dev.astype(jnp.float32))
        return jnp.where(live_dev[:, None, None], prod, 0.0)

    contrib = lax.map(one_device, (jnp.moveaxis(zone_flat, 1, 0), src, wts, live))
    target = (owners[:, 0] * HOST_BLK + slots).astype(jnp.int32)
    host_adjoint = jax.ops.segment_sum(contrib.reshape(N_GY * NBLK, LEV, HB), target, num_segments=N_GY * HOST_BLK)
    return field, host_adjoint
```

```python
import functools

import jax
import jax.numpy as jnp
from jax import lax
from jax.experimental import pallas as pl
from jax.experimental.pallas import tpu as pltpu
from jax.sharding import PartitionSpec as P

ZW = 16
SUB = 4
HOST_BLK = 32
STEP_BLOCKS = 16
MESH = pl.DeviceIdType.MESH


def from_behind(value, axis, steps):
    count = lax.axis_size(axis)
    initial, last = (max(0, -steps), min(count, count - steps))
    return lax.ppermute(value, axis, [(source, source + steps) for source in range(initial, last)])


def davies(dist):
    frac = 1.0 - dist.astype(jnp.float32) / ZW
    return frac * frac


def sideways(field, k_west, k_east):
    g_west = k_west * field
    g_east = k_east * field
    zero_col = jnp.zeros_like(field[:, :, :1])
    left_part = jnp.concatenate([g_west[:, :, 1:], zero_col], 2)
    right_part = jnp.concatenate([zero_col, g_east[:, :, :-1]], 2)
    return (left_part, right_part)


def split_dot(onehot, x):
    hi = x.astype(jnp.bfloat16)
    lo = (x - hi.astype(jnp.float32)).astype(jnp.bfloat16)
    return jnp.dot(onehot, hi, preferred_element_type=jnp.float32) + jnp.dot(
        onehot, lo, preferred_element_type=jnp.float32
    )


def contrib_kernel(
    owner_count, capacity, width, src_ref, w_ref, left_ref, right_ref, dleft_ref, dright_ref,
    owner_ref, slot_ref, count_ref, packed_ref, table, contrib,
):
    step = pl.program_id(0)
    nblk = owner_ref.shape[1]
    levels, rows, lanes = left_ref.shape
    per = lanes // (2 * ZW)

    @pl.when(step == 0)
    def _():
        lane = lax.broadcasted_iota(jnp.int32, (levels, lanes), 1)
        for q in range(rows // per):
            tile = jnp.zeros((levels, lanes), jnp.float32)
            for i in range(per):
                r = q * per + i
                zl = davies(dleft_ref[r : r + 1, :]) * left_ref[:, r, :]
                zr = davies(dright_ref[r : r + 1, :]) * right_ref[:, r, :]
                both = jnp.where(lane < lanes // 2, zl, zr)
                both = pltpu.roll(both, (ZW + 2 * ZW * i) % lanes, 1)
                tile = jnp.where(lane // (2 * ZW) == i, both, tile)
            table[q] = tile

    src = src_ref[...]
    row = src // width
    col = src % width
    spot = jnp.where(col < ZW, col + ZW, col - (width - ZW)) + (row % per) * (2 * ZW)
    group = row // per
    for j in range(src.shape[0]):
        at = jnp.broadcast_to(spot[j : j + 1, :], (levels, lanes))
        which = jnp.broadcast_to(group[j : j + 1, :], (levels, lanes))
        value = jnp.take_along_axis(table[0], at, axis=1)
        for q in range(1, rows // per):
            value = jnp.where(which == q, jnp.take_along_axis(table[q], at, axis=1), value)
        out = jnp.dot(value.astype(jnp.bfloat16), w_ref[j], preferred_element_type=jnp.float32)
        contrib[pl.ds(step * STEP_BLOCKS + j, levels, stride=nblk), :] = out

    @pl.when(step == pl.num_programs(0) - 1)
    def _():
        owner = owner_ref[...]
        names = owner == lax.broadcasted_iota(jnp.int32, (owner_count, nblk), 0)
        onehot = jnp.where(names, 1.0, 0.0)
        earlier = lax.broadcasted_iota(jnp.int32, (nblk, nblk), 0) < lax.broadcasted_iota(
            jnp.int32, (nblk, nblk), 1
        )
        before = jnp.dot(
            onehot.astype(jnp.bfloat16),
            jnp.where(earlier, 1.0, 0.0).astype(jnp.bfloat16),
            preferred_element_type=jnp.float32,
        )
        rank = jnp.sum(onehot * before, axis=0, keepdims=True).astype(jnp.int32)
        target = owner * capacity + rank
        live = lax.broadcasted_iota(jnp.int32, (1, nblk), 1) < count_ref[0]
        target = jnp.where(live, target, -1)
        places = owner_count * capacity
        hit = lax.broadcasted_iota(jnp.int32, (places, nblk), 0) == target
        place = jnp.where(hit, 1.0, 0.0).astype(jnp.bfloat16)
        for l in range(levels):
            packed_ref[l] = split_dot(place, contrib[l * nblk : (l + 1) * nblk, :])
        ids = jnp.sum(jnp.where(hit, slot_ref[...].astype(jnp.float32), 0.0), axis=1, keepdims=True)
        packed_ref[levels] = jnp.broadcast_to(ids, (places, packed_ref.shape[2]))


def exchange_kernel(
    n, capacity, packed_ref, adjoint_ref, coeffs_ref, dist_ref, grad_ref, host_ref,
    field, coef, turned, received, halo_send, halo_recv, own_sem, send_sem, recv_sem,
):
    me = lax.axis_index("gy")
    rows, width = dist_ref.shape
    levels = adjoint_ref.shape[0] // rows
    pad = 8
    barrier = pltpu.get_barrier_semaphore()
    for k in range(1, n):
        pl.semaphore_signal(barrier, inc=1, device_id={"gy": lax.rem(me + k, n)}, device_id_type=MESH)

    own = pltpu.make_async_copy(coeffs_ref, coef.at[:, pad : pad + rows, :], own_sem)
    own.start()

    tiles = width // 128
    for c in range(tiles):
        turned[c] = adjoint_ref[:, c * 128 : (c + 1) * 128]

    @pl.loop(0, rows)
    def _(r):
        keep = 1.0 - davies(dist_ref[pl.ds(r, 1), :])
        for c in range(tiles):
            cut = slice(c * 128, (c + 1) * 128)
            field[r + SUB, :, cut] = keep[:, cut] * turned[c, pl.ds(r, levels, stride=rows), :]

    pl.semaphore_wait(barrier, n - 1)

    def halo(up):
        to = {"gy": me - 1 if up else me + 1}
        at = 0 if up else 1
        first = SUB if up else rows
        return [
            pltpu.make_async_remote_copy(
                src_ref=field.at[first : first + SUB],
                dst_ref=field.at[rows + SUB : rows + 2 * SUB] if up else field.at[0:SUB],
                send_sem=halo_send.at[at, 0],
                recv_sem=halo_recv.at[at, 0],
                device_id=to,
                device_id_type=MESH,
            ),
            pltpu.make_async_remote_copy(
                src_ref=coeffs_ref.at[:, 0:pad, :] if up else coeffs_ref.at[:, rows - pad : rows, :],
                dst_ref=coef.at[:, rows + pad :, :] if up else coef.at[:, 0:pad, :],
                send_sem=halo_send.at[at, 1],
                recv_sem=halo_recv.at[at, 1],
                device_id=to,
                device_id_type=MESH,
            ),
        ]

    up, down = halo(True), halo(False)

    @pl.when(me > 0)
    def _():
        for copy in up:
            copy.start()

    @pl.when(me < n - 1)
    def _():
        for copy in down:
            copy.start()

    copies = []
    for k in range(1, n):
        to = lax.rem(me + k, n)
        copy = pltpu.make_async_remote_copy(
            src_ref=packed_ref.at[:, pl.ds(pl.multiple_of(to * capacity, 8), capacity), :],
            dst_ref=received.at[:, pl.ds(pl.multiple_of(me * capacity, 8), capacity), :],
            send_sem=send_sem.at[k - 1],
            recv_sem=recv_sem.at[k - 1],
            device_id={"gy": to},
            device_id_type=MESH,
        )
        copy.start()
        copies.append(copy)
    mine = pl.ds(pl.multiple_of(me * capacity, 8), capacity)
    received[:, mine, :] = packed_ref[:, mine, :]

    @pl.when(me == 0)
    def _():
        field[0:SUB] = jnp.zeros((SUB, levels, width), jnp.float32)
        coef[:, 0:pad, :] = jnp.zeros((4, pad, width), jnp.float32)

    @pl.when(me == n - 1)
    def _():
        field[rows + SUB :] = jnp.zeros((SUB, levels, width), jnp.float32)
        coef[:, rows + pad :, :] = jnp.zeros((4, pad, width), jnp.float32)

    own.wait()

    @pl.when(me > 0)
    def _():
        for copy in up:
            copy.wait_send()
        for copy in down:
            copy.wait_recv()

    @pl.when(me < n - 1)
    def _():
        for copy in down:
            copy.wait_send()
        for copy in up:
            copy.wait_recv()

    column = lax.broadcasted_iota(jnp.int32, (levels, width), 1)

    def k_row(which, r):
        return jnp.broadcast_to(coef[which, pl.ds(r + pad - SUB, 1), :], (levels, width))

    for step in range(SUB):
        low, high = step + 1, rows + 2 * SUB - 1 - step

        def body(r, carry):
            from_above, here = carry
            below = field[r + 1]
            k_n, k_s, k_w, k_e = (k_row(i, r) for i in range(4))
            g_west = pltpu.roll(k_w * here, width - 1, 1)
            g_east = pltpu.roll(k_e * here, 1, 1)
            g_west = jnp.where(column == width - 1, 0.0, g_west)
            g_east = jnp.where(column == 0, 0.0, g_east)
            new = here * (1.0 - (k_n + k_s + k_w + k_e)) + k_row(0, r + 1) * below
            new = new + from_above + g_west + g_east
            if step == SUB - 1:
                for c in range(tiles):
                    turned[c, pl.ds(r - SUB, levels, stride=rows), :] = new[:, c * 128 : (c + 1) * 128]
            else:
                field[r] = new
            return (k_s * here, below)

        lax.fori_loop(low, high, body, (k_row(1, low - 1) * field[low - 1], field[low]))

    for c in range(tiles):
        grad_ref[:, c * 128 : (c + 1) * 128] = turned[c]
    for copy in copies:
        copy.wait()
    ids = received[levels]
    named = jnp.where(ids == lax.broadcasted_iota(jnp.int32, ids.shape, 1).astype(jnp.float32), 1.0, 0.0)
    place = named.T[:HOST_BLK].astype(jnp.bfloat16)
    for l in range(levels):
        host_ref[pl.ds(l, HOST_BLK, stride=levels), :] = split_dot(place, received[l])


def fused(n, capacity, adjoint, coeffs, dist, sources, weights, owners, slots, counts):
    levels, rows, width = adjoint.shape
    nblk, block = sources.shape
    host_width = weights.shape[2]
    places = n * capacity
    last = width // 128 - 1
    whole = lambda shape: pl.BlockSpec(shape, lambda i: (0,) * len(shape))
    packed = pl.pallas_call(
        functools.partial(contrib_kernel, n, capacity, width),
        grid=(nblk // STEP_BLOCKS,),
        out_shape=jax.ShapeDtypeStruct((levels + 1, places, host_width), jnp.float32),
        in_specs=[
            pl.BlockSpec((STEP_BLOCKS, block), lambda i: (i, 0)),
            pl.BlockSpec((STEP_BLOCKS, block, host_width), lambda i: (i, 0, 0)),
            pl.BlockSpec((levels, rows, 128), lambda i: (0, 0, 0)),
            pl.BlockSpec((levels, rows, 128), lambda i: (0, 0, last)),
            pl.BlockSpec((rows, 128), lambda i: (0, 0)),
            pl.BlockSpec((rows, 128), lambda i: (0, last)),
            whole((1, nblk)),
            whole((1, nblk)),
            pl.BlockSpec(memory_space=pltpu.SMEM),
        ],
        out_specs=whole((levels + 1, places, host_width)),
        scratch_shapes=[
            pltpu.VMEM((rows * 2 * ZW // 128, levels, 128), jnp.float32),
            pltpu.VMEM((levels * nblk, host_width), jnp.float32),
        ],
        compiler_params=pltpu.CompilerParams(vmem_limit_bytes=24 * 2**20),
        name="contributions",
    )(sources, weights, adjoint, adjoint, dist, dist, owners.reshape(1, nblk), slots.reshape(1, nblk), counts)
    vmem = pl.BlockSpec(memory_space=pltpu.VMEM)
    grad, host = pl.pallas_call(
        functools.partial(exchange_kernel, n, capacity),
        out_shape=[
            jax.ShapeDtypeStruct((levels * rows, width), jnp.float32),
            jax.ShapeDtypeStruct((HOST_BLK * levels, host_width), jnp.float32),
        ],
        in_specs=[vmem] * 4,
        out_specs=[vmem, vmem],
        scratch_shapes=[
            pltpu.VMEM((rows + 2 * SUB, levels, width), jnp.float32),
            pltpu.VMEM((4, rows + 16, width), jnp.float32),
            pltpu.VMEM((width // 128, levels * rows, 128), jnp.float32),
            pltpu.VMEM((levels + 1, places, host_width), jnp.float32),
            pltpu.SemaphoreType.DMA((2, 2)),
            pltpu.SemaphoreType.DMA((2, 2)),
            pltpu.SemaphoreType.DMA,
            pltpu.SemaphoreType.DMA((n - 1,)),
            pltpu.SemaphoreType.DMA((n - 1,)),
        ],
        compiler_params=pltpu.CompilerParams(
            collective_id=0, has_side_effects=True, vmem_limit_bytes=24 * 2**20
        ),
        name="exchange",
    )(packed, adjoint.reshape(levels * rows, width), coeffs, dist)
    return grad.reshape(levels, rows, width), host.reshape(HOST_BLK, levels, host_width)


def local(adjoint, coeffs, dist, sources, weights, owners, slots, counts):
    levels, rows, width = adjoint.shape
    nblk = sources.shape[0]
    host_width = weights.shape[2]
    owner_count = lax.axis_size("gy")
    capacity = max(2, (2 * nblk + owner_count - 1) // owner_count)
    if capacity % 8 == 0:
        return fused(owner_count, capacity, adjoint, coeffs, dist, sources, weights, owners, slots, counts)
    relax = davies(dist)
    k_north, k_south, k_west, k_east = (coeffs[0], coeffs[1], coeffs[2], coeffs[3])
    total = k_north + k_south + k_west + k_east
    zone = (relax * adjoint).reshape(levels, rows * width)
    values = jnp.take(zone, sources, axis=1).astype(jnp.bfloat16)
    contrib = jnp.einsum("lbk,bkh->blh", values, weights, preferred_element_type=jnp.float32)
    live = lax.iota(jnp.int32, nblk) < counts[0]
    flat_contrib = jnp.where(live[:, None, None], contrib, 0.0).reshape(nblk, levels * host_width)
    owner_ids = owners[:, 0]
    onehot = (owner_ids[:, None] == lax.iota(jnp.int32, owner_count)[None, :]).astype(jnp.int32)
    before = jnp.cumsum(onehot, axis=0) - onehot
    position = jnp.sum(before * onehot, axis=1)
    target = owner_ids * capacity + position
    packed = (
        jnp.zeros((owner_count * capacity, levels * host_width), jnp.float32)
        .at[target]
        .set(flat_contrib)
    )
    block_ids = (
        jnp.full((owner_count * capacity,), -1.0, jnp.float32)
        .at[target]
        .set(jnp.where(live, slots.astype(jnp.float32), -1.0))
    )
    received, got_ids = (
        lax.all_to_all(
            packed.reshape(owner_count, capacity, levels * host_width),
            "gy",
            split_axis=0,
            concat_axis=0,
            tiled=True,
        ),
        lax.all_to_all(
            block_ids.reshape(owner_count, capacity), "gy", split_axis=0, concat_axis=0, tiled=True
        ),
    )
    flat_ids = got_ids.reshape(-1).astype(jnp.int32)
    flat_ids = jnp.where(flat_ids >= 0, flat_ids, HOST_BLK)
    buffer = jnp.zeros((HOST_BLK + 1, levels * host_width), jnp.float32)
    host = buffer.at[flat_ids].add(received.reshape(owner_count * capacity, levels * host_width))[
        :HOST_BLK
    ]
    host_adjoint = host.reshape(HOST_BLK, levels, host_width)
    field = (1.0 - relax) * adjoint
    for step in range(SUB):
        g_north = k_north * field
        g_south = k_south * field
        below = from_behind(g_north[:, :1, :], "gy", -1)
        above = from_behind(g_south[:, -1:, :], "gy", 1)
        upper = jnp.concatenate([g_north[:, 1:, :], below], 1)
        lower = jnp.concatenate([above, g_south[:, :-1, :]], 1)
        left_part, right_part = sideways(field, k_west, k_east)
        field = field * (1.0 - total) + upper + lower + left_part + right_part
    return (field, host_adjoint)


def solution(mesh):
    placed = (
        P("groups", "gy", None),
        P(None, "gy", None),
        P("gy", None),
        P("gy", None),
        P("gy", None, None),
        P("gy", None),
        P("gy"),
        P("gy"),
    )
    return jax.shard_map(
        local,
        mesh=mesh,
        in_specs=placed,
        out_specs=(P("groups", "gy", None), P("gy", "groups", None)),
        check_vma=False,
    )
```

```python
import functools

import jax
import jax.numpy as jnp
from jax import lax
from jax.experimental import pallas as pl
from jax.experimental.pallas import tpu as pltpu
from jax.sharding import PartitionSpec as P

ZW = 16
SUB = 4
HOST_BLK = 32
STEP_BLOCKS = 16
W_PARTS = 4
CHUNK = 2
MESH = pl.DeviceIdType.MESH


def from_behind(value, axis, steps):
    count = lax.axis_size(axis)
    initial, last = (max(0, -steps), min(count, count - steps))
    return lax.ppermute(value, axis, [(source, source + steps) for source in range(initial, last)])


def davies(dist):
    frac = 1.0 - dist.astype(jnp.float32) / ZW
    return frac * frac


def sideways(field, k_west, k_east):
    g_west = k_west * field
    g_east = k_east * field
    zero_col = jnp.zeros_like(field[:, :, :1])
    left_part = jnp.concatenate([g_west[:, :, 1:], zero_col], 2)
    right_part = jnp.concatenate([zero_col, g_east[:, :, :-1]], 2)
    return (left_part, right_part)


def split_dot(onehot, x):
    hi = x.astype(jnp.bfloat16)
    lo = (x - hi.astype(jnp.float32)).astype(jnp.bfloat16)
    return jnp.dot(onehot, hi, preferred_element_type=jnp.float32) + jnp.dot(
        onehot, lo, preferred_element_type=jnp.float32
    )


def fused_kernel(
    n, sizes, adjoint_hbm, coeffs_hbm, dist_hbm, sources_hbm, weights_hbm, owner_ref, slot_ref, count_ref,
    grad_ref, host_ref,
    adjoint_ref, dist_ref, src_ref, w_ref, table, contrib, field, coef, stage, got_stage, turned,
    dense, got_core, half, got_x, quarter, got_z,
    in_sem, w_sem, halo_send, halo_recv, core_send, core_recv, x_send, x_recv, z_send, z_recv,
):
    nz, nx, nc = sizes
    me = lax.axis_index("gy")
    my_z, my_x, my_c = me // (nx * nc), (me // nc) % nx, me % nc
    rows, width = dist_ref.shape
    levels = adjoint_ref.shape[0] // rows
    nblk, lanes = src_ref.shape
    tiles = width // lanes
    pad = 8
    per = lanes // (2 * ZW)

    def at_gy(z, x, c):
        return {"gy": (z * nx + x) * nc + c}

    core_peer = at_gy(my_z, my_x, 1 - my_c)
    x_peer = at_gy(my_z, 1 - my_x, my_c)
    z_peers = [at_gy(lax.rem(my_z + k, nz), my_x, my_c) for k in range(1, nz)]

    barrier = pltpu.get_barrier_semaphore()
    around = [{"gy": lax.rem(me + n - 1, n)}, {"gy": lax.rem(me + 1, n)}]
    partners = [core_peer, x_peer] + z_peers + around
    for peer in partners:
        pl.semaphore_signal(barrier, inc=1, device_id=peer, device_id_type=MESH)

    loads = [
        pltpu.make_async_copy(source, target, in_sem.at[i])
        for i, (source, target) in enumerate(
            [
                (dist_hbm, dist_ref),
                (adjoint_hbm, adjoint_ref),
                (coeffs_hbm, coef.at[:, pad : pad + rows, :]),
                (sources_hbm, src_ref),
            ]
        )
    ]
    for load in loads:
        load.start()
    w_loads = []
    for i in range(W_PARTS):
        part = pl.ds(i * (nblk // W_PARTS), nblk // W_PARTS)
        w_loads.append(pltpu.make_async_copy(weights_hbm.at[part], w_ref.at[part], w_sem.at[i]))
        w_loads[-1].start()

    for load in loads:
        load.wait()
    for c in range(tiles):
        turned[c] = adjoint_ref[:, c * lanes : (c + 1) * lanes]

    @pl.loop(0, rows)
    def _(r):
        keep = 1.0 - davies(dist_ref[pl.ds(r, 1), :])
        for c in range(tiles):
            cut = slice(c * lanes, (c + 1) * lanes)
            field[r + SUB, :, cut] = keep[:, cut] * turned[c, pl.ds(r, levels, stride=rows), :]

    for i in range(4):
        spot = slice(i % 2 * SUB, (i % 2 + 1) * SUB)
        stage[0, i // 2, spot] = coef[i, pad : pad + SUB, :]
        stage[1, i // 2, spot] = coef[i, pad + rows - SUB : pad + rows, :]

    pl.semaphore_wait(barrier, len(partners))

    def halo(at):
        to = {"gy": me - 1 if at == 0 else me + 1}
        first = SUB if at == 0 else rows
        land = rows + SUB if at == 0 else 0
        return [
            pltpu.make_async_remote_copy(
                src_ref=field.at[first : first + SUB],
                dst_ref=field.at[land : land + SUB],
                send_sem=halo_send.at[at, 0],
                recv_sem=halo_recv.at[at, 0],
                device_id=to,
                device_id_type=MESH,
            ),
            pltpu.make_async_remote_copy(
                src_ref=stage.at[at],
                dst_ref=got_stage.at[at],
                send_sem=halo_send.at[at, 1],
                recv_sem=halo_recv.at[at, 1],
                device_id=to,
                device_id_type=MESH,
            ),
        ]

    up, down = halo(0), halo(1)

    @pl.when(me > 0)
    def _():
        for copy in up:
            copy.start()

    @pl.when(me < n - 1)
    def _():
        for copy in down:
            copy.start()

    lane = lax.broadcasted_iota(jnp.int32, (levels, lanes), 1)
    for q in range(rows // per):
        tile = jnp.zeros((levels, lanes), jnp.float32)
        for i in range(per):
            r = q * per + i
            z_left = davies(dist_ref[r : r + 1, :lanes]) * turned[0, pl.ds(r, levels, stride=rows), :]
            z_right = davies(dist_ref[r : r + 1, width - lanes :]) * turned[tiles - 1, pl.ds(r, levels, stride=rows), :]
            both = jnp.where(lane < lanes // 2, z_left, z_right)
            both = pltpu.roll(both, (ZW + 2 * ZW * i) % lanes, 1)
            tile = jnp.where((lane >= 2 * ZW * i) & (lane < 2 * ZW * (i + 1)), both, tile)
        table[q] = tile

    for part in range(W_PARTS):
        w_loads[part].wait()

        @pl.loop(part * (nblk // W_PARTS // STEP_BLOCKS), (part + 1) * (nblk // W_PARTS // STEP_BLOCKS))
        def _(step):
            base = pl.multiple_of(step * STEP_BLOCKS, STEP_BLOCKS)
            src = src_ref[pl.ds(base, STEP_BLOCKS), :]
            row = src // width
            col = src - row * width
            spot = jnp.where(col < ZW, col + ZW, col - (width - ZW)) + (row % per) * (2 * ZW)
            group = row // per
            for j in range(STEP_BLOCKS):
                at = jnp.broadcast_to(spot[j : j + 1, :], (levels, lanes))
                which = jnp.broadcast_to(group[j : j + 1, :], (levels, lanes))
                value = jnp.take_along_axis(table[0], at, axis=1)
                for q in range(1, rows // per):
                    value = jnp.where(which == q, jnp.take_along_axis(table[q], at, axis=1), value)
                out = jnp.dot(value.astype(jnp.bfloat16), w_ref[base + j], preferred_element_type=jnp.float32)
                contrib[pl.ds(base + j, levels, stride=nblk), :] = out

    owner = owner_ref[...]
    own_z, own_x, own_c = owner // (nx * nc), (owner // nc) % nx, owner % nc
    target = ((own_c * nx + own_x) * nz + own_z) * HOST_BLK + slot_ref[...]
    live = lax.broadcasted_iota(jnp.int32, (1, nblk), 1) < count_ref[0]
    target = jnp.where(live, target, -1)
    hosts = n * HOST_BLK
    hit = lax.broadcasted_iota(jnp.int32, (hosts, nblk), 0) == target
    place = jnp.where(hit, 1.0, 0.0).astype(jnp.bfloat16)

    count = levels // CHUNK
    part_of = lambda i: pl.ds(i * CHUNK, CHUNK)
    sent = []
    for i in range(count):
        for l in range(i * CHUNK, (i + 1) * CHUNK):
            full = split_dot(place, contrib[l * nblk : (l + 1) * nblk, :])
            dense[l] = full.reshape(nc, nx, nz, HOST_BLK, lanes)
        sent.append(
            pltpu.make_async_remote_copy(
                src_ref=dense.at[part_of(i), 1 - my_c],
                dst_ref=got_core.at[part_of(i)],
                send_sem=core_send.at[i],
                recv_sem=core_recv.at[i],
                device_id=core_peer,
                device_id_type=MESH,
            )
        )
        sent[-1].start()
    for i in range(count):
        sent[i].wait()
        half[part_of(i)] = dense[part_of(i), my_c] + got_core[part_of(i)]
        sent.append(
            pltpu.make_async_remote_copy(
                src_ref=half.at[part_of(i), 1 - my_x],
                dst_ref=got_x.at[part_of(i)],
                send_sem=x_send.at[i],
                recv_sem=x_recv.at[i],
                device_id=x_peer,
                device_id_type=MESH,
            )
        )
        sent[-1].start()

    @pl.when(me == 0)
    def _():
        field[0:SUB] = jnp.zeros((SUB, levels, width), jnp.float32)
        got_stage[1] = jnp.zeros(got_stage.shape[1:], jnp.float32)

    @pl.when(me == n - 1)
    def _():
        field[rows + SUB :] = jnp.zeros((SUB, levels, width), jnp.float32)
        got_stage[0] = jnp.zeros(got_stage.shape[1:], jnp.float32)

    @pl.when(me > 0)
    def _():
        for copy in up:
            copy.wait_send()
        for copy in down:
            copy.wait_recv()

    @pl.when(me < n - 1)
    def _():
        for copy in down:
            copy.wait_send()
        for copy in up:
            copy.wait_recv()

    for i in range(4):
        spot = slice(i % 2 * SUB, (i % 2 + 1) * SUB)
        coef[i, pad - SUB : pad, :] = got_stage[1, i // 2, spot]
        coef[i, pad + rows : pad + rows + SUB, :] = got_stage[0, i // 2, spot]

    column = lax.broadcasted_iota(jnp.int32, (levels, width), 1)

    def k_row(which, r):
        return jnp.broadcast_to(coef[which, pl.ds(r + pad - SUB, 1), :], (levels, width))

    def sweep(step):
        low, high = step + 1, rows + 2 * SUB - 1 - step

        def body(r, carry):
            from_above, here = carry
            below = field[r + 1]
            k_n, k_s, k_w, k_e = (k_row(i, r) for i in range(4))
            g_west = pltpu.roll(k_w * here, width - 1, 1)
            g_east = pltpu.roll(k_e * here, 1, 1)
            g_west = jnp.where(column == width - 1, 0.0, g_west)
            g_east = jnp.where(column == 0, 0.0, g_east)
            new = here * (1.0 - (k_n + k_s + k_w + k_e)) + k_row(0, r + 1) * below
            new = new + from_above + g_west + g_east
            if step == SUB - 1:
                for c in range(tiles):
                    turned[c, pl.ds(r - SUB, levels, stride=rows), :] = new[:, c * lanes : (c + 1) * lanes]
            else:
                field[r] = new
            return (k_s * here, below)

        lax.fori_loop(low, high, body, (k_row(1, low - 1) * field[low - 1], field[low]))

    z_sent = []

    def along_z(i):
        sent[count + i].wait()
        quarter[part_of(i)] = half[part_of(i), my_x] + got_x[part_of(i)]
        for k in range(1, nz):
            z_sent.append(
                pltpu.make_async_remote_copy(
                    src_ref=quarter.at[part_of(i), lax.rem(my_z + k, nz)],
                    dst_ref=got_z.at[k - 1, part_of(i)],
                    send_sem=z_send.at[i, k - 1],
                    recv_sem=z_recv.at[i, k - 1],
                    device_id=z_peers[k - 1],
                    device_id_type=MESH,
                )
            )
            z_sent[-1].start()

    done = 0
    for step in range(SUB):
        sweep(step)
        upto = count - 1 if step == SUB - 1 else (step + 1) * (count - 1) // SUB
        for i in range(done, upto):
            along_z(i)
        done = upto
    for c in range(tiles):
        grad_ref[:, c * lanes : (c + 1) * lanes] = turned[c]
    along_z(count - 1)
    for i in range(count):
        for copy in z_sent[i * (nz - 1) : (i + 1) * (nz - 1)]:
            copy.wait()
        for l in range(i * CHUNK, (i + 1) * CHUNK):
            total = quarter[l, my_z]
            for k in range(nz - 1):
                total = total + got_z[k, l]
            host_ref[pl.ds(l, HOST_BLK, stride=levels), :] = total


def fused(n, sizes, adjoint, coeffs, dist, sources, weights, owners, slots, counts):
    levels, rows, width = adjoint.shape
    nblk, block = sources.shape
    lanes = weights.shape[2]
    nz, nx, nc = sizes
    count = levels // CHUNK
    f32 = lambda *shape: pltpu.VMEM(shape, jnp.float32)
    dma = lambda *shape: pltpu.SemaphoreType.DMA(shape)
    hbm = pl.BlockSpec(memory_space=pltpu.HBM)
    vmem = pl.BlockSpec(memory_space=pltpu.VMEM)
    grad, host = pl.pallas_call(
        functools.partial(fused_kernel, n, sizes),
        out_shape=[
            jax.ShapeDtypeStruct((levels * rows, width), jnp.float32),
            jax.ShapeDtypeStruct((HOST_BLK * levels, lanes), jnp.float32),
        ],
        in_specs=[hbm] * 5 + [vmem] * 2 + [pl.BlockSpec(memory_space=pltpu.SMEM)],
        out_specs=[vmem, vmem],
        scratch_shapes=[
            f32(levels * rows, width),
            pltpu.VMEM((rows, width), jnp.int32),
            pltpu.VMEM((nblk, block), jnp.int32),
            pltpu.VMEM((nblk, block, lanes), jnp.bfloat16),
            f32(rows * 2 * ZW // lanes, levels, lanes),
            f32(levels * nblk, lanes),
            f32(rows + 2 * SUB, levels, width),
            f32(4, rows + 16, width),
            f32(2, 2, 2 * SUB, width),
            f32(2, 2, 2 * SUB, width),
            f32(width // lanes, levels * rows, lanes),
            f32(levels, nc, nx, nz, HOST_BLK, lanes),
            f32(levels, nx, nz, HOST_BLK, lanes),
            f32(levels, nx, nz, HOST_BLK, lanes),
            f32(levels, nz, HOST_BLK, lanes),
            f32(levels, nz, HOST_BLK, lanes),
            f32(nz - 1, levels, HOST_BLK, lanes),
            dma(4),
            dma(W_PARTS),
            dma(2, 2),
            dma(2, 2),
            dma(count),
            dma(count),
            dma(count),
            dma(count),
            dma(count, nz - 1),
            dma(count, nz - 1),
        ],
        compiler_params=pltpu.CompilerParams(
            collective_id=0, has_side_effects=True, vmem_limit_bytes=62 * 2**20
        ),
        name="fused",
    )(
        adjoint.reshape(levels * rows, width), coeffs, dist, sources, weights,
        owners.reshape(1, nblk), slots.reshape(1, nblk), counts,
    )
    return grad.reshape(levels, rows, width), host.reshape(HOST_BLK, levels, lanes)


def local(adjoint, coeffs, dist, sources, weights, owners, slots, counts):
    levels, rows, width = adjoint.shape
    nblk = sources.shape[0]
    host_width = weights.shape[2]
    owner_count = lax.axis_size("gy")
    capacity = max(2, (2 * nblk + owner_count - 1) // owner_count)
    if owner_count == 16:
        return fused(owner_count, (4, 2, 2), adjoint, coeffs, dist, sources, weights, owners, slots, counts)
    relax = davies(dist)
    k_north, k_south, k_west, k_east = (coeffs[0], coeffs[1], coeffs[2], coeffs[3])
    total = k_north + k_south + k_west + k_east
    zone = (relax * adjoint).reshape(levels, rows * width)
    values = jnp.take(zone, sources, axis=1).astype(jnp.bfloat16)
    contrib = jnp.einsum("lbk,bkh->blh", values, weights, preferred_element_type=jnp.float32)
    live = lax.iota(jnp.int32, nblk) < counts[0]
    flat_contrib = jnp.where(live[:, None, None], contrib, 0.0).reshape(nblk, levels * host_width)
    owner_ids = owners[:, 0]
    onehot = (owner_ids[:, None] == lax.iota(jnp.int32, owner_count)[None, :]).astype(jnp.int32)
    before = jnp.cumsum(onehot, axis=0) - onehot
    position = jnp.sum(before * onehot, axis=1)
    target = owner_ids * capacity + position
    packed = (
        jnp.zeros((owner_count * capacity, levels * host_width), jnp.float32)
        .at[target]
        .set(flat_contrib)
    )
    block_ids = (
        jnp.full((owner_count * capacity,), -1.0, jnp.float32)
        .at[target]
        .set(jnp.where(live, slots.astype(jnp.float32), -1.0))
    )
    received, got_ids = (
        lax.all_to_all(
            packed.reshape(owner_count, capacity, levels * host_width),
            "gy",
            split_axis=0,
            concat_axis=0,
            tiled=True,
        ),
        lax.all_to_all(
            block_ids.reshape(owner_count, capacity), "gy", split_axis=0, concat_axis=0, tiled=True
        ),
    )
    flat_ids = got_ids.reshape(-1).astype(jnp.int32)
    flat_ids = jnp.where(flat_ids >= 0, flat_ids, HOST_BLK)
    buffer = jnp.zeros((HOST_BLK + 1, levels * host_width), jnp.float32)
    host = buffer.at[flat_ids].add(received.reshape(owner_count * capacity, levels * host_width))[
        :HOST_BLK
    ]
    host_adjoint = host.reshape(HOST_BLK, levels, host_width)
    field = (1.0 - relax) * adjoint
    for step in range(SUB):
        g_north = k_north * field
        g_south = k_south * field
        below = from_behind(g_north[:, :1, :], "gy", -1)
        above = from_behind(g_south[:, -1:, :], "gy", 1)
        upper = jnp.concatenate([g_north[:, 1:, :], below], 1)
        lower = jnp.concatenate([above, g_south[:, :-1, :]], 1)
        left_part, right_part = sideways(field, k_west, k_east)
        field = field * (1.0 - total) + upper + lower + left_part + right_part
    return (field, host_adjoint)


def solution(mesh):
    placed = (
        P("groups", "gy", None),
        P(None, "gy", None),
        P("gy", None),
        P("gy", None),
        P("gy", None, None),
        P("gy", None),
        P("gy"),
        P("gy"),
    )
    return jax.shard_map(
        local,
        mesh=mesh,
        in_specs=placed,
        out_specs=(P("groups", "gy", None), P("gy", "groups", None)),
        check_vma=False,
    )
```

```python
import functools

import jax
import jax.numpy as jnp
from jax import lax
from jax.experimental import pallas as pl
from jax.experimental.pallas import tpu as pltpu
from jax.sharding import PartitionSpec as P

ZW = 16
SUB = 4
HOST_BLK = 32
STEP_BLOCKS = 16
W_PARTS = 4
Z_AFTER = (3, 6, 8)
MESH = pl.DeviceIdType.MESH


def from_behind(value, axis, steps):
    count = lax.axis_size(axis)
    initial, last = (max(0, -steps), min(count, count - steps))
    return lax.ppermute(value, axis, [(source, source + steps) for source in range(initial, last)])


def davies(dist):
    frac = 1.0 - dist.astype(jnp.float32) / ZW
    return frac * frac


def sideways(field, k_west, k_east):
    g_west = k_west * field
    g_east = k_east * field
    zero_col = jnp.zeros_like(field[:, :, :1])
    left_part = jnp.concatenate([g_west[:, :, 1:], zero_col], 2)
    right_part = jnp.concatenate([zero_col, g_east[:, :, :-1]], 2)
    return (left_part, right_part)


def split_dot(onehot, x):
    hi = x.astype(jnp.bfloat16)
    lo = (x - hi.astype(jnp.float32)).astype(jnp.bfloat16)
    return jnp.dot(onehot, hi, preferred_element_type=jnp.float32) + jnp.dot(
        onehot, lo, preferred_element_type=jnp.float32
    )


def chunks_of(levels):
    sizes = [2] * (levels // 2 - 1) + [1, 1]
    return [(sum(sizes[:i]), size) for i, size in enumerate(sizes)]


def deliver_kernel(grad_in, host_in, grad_ref, host_ref, sem):
    copies = [
        pltpu.make_async_copy(grad_in, grad_ref, sem.at[0]),
        pltpu.make_async_copy(host_in, host_ref, sem.at[1]),
    ]
    for copy in copies:
        copy.start()
    for copy in copies:
        copy.wait()


def fused_kernel(
    n, sizes, adjoint_hbm, coeffs_hbm, dist_hbm, sources_hbm, weights_hbm, owner_ref, slot_ref, count_ref,
    grad_ref, host_ref,
    adjoint_ref, dist_ref, src_ref, w_ref, table, contrib, field, coef, stage, got_stage, turned,
    dense, got_core, half, got_x, quarter, got_z,
    in_sem, w_sem, out_sem, halo_send, halo_recv, core_send, core_recv, x_send, x_recv, z_send, z_recv,
):
    nz, nx, nc = sizes
    me = lax.axis_index("gy")
    my_z, my_x, my_c = me // (nx * nc), (me // nc) % nx, me % nc
    rows, width = dist_ref.shape
    levels = adjoint_ref.shape[0] // rows
    nblk, lanes = src_ref.shape
    tiles = width // lanes
    pad = 8
    per = lanes // (2 * ZW)

    def at_gy(z, x, c):
        return {"gy": (z * nx + x) * nc + c}

    core_peer = at_gy(my_z, my_x, 1 - my_c)
    x_peer = at_gy(my_z, 1 - my_x, my_c)
    z_peers = [at_gy(lax.rem(my_z + k, nz), my_x, my_c) for k in range(1, nz)]

    barrier = pltpu.get_barrier_semaphore()
    around = [{"gy": lax.rem(me + n - 1, n)}, {"gy": lax.rem(me + 1, n)}]
    partners = [core_peer, x_peer] + z_peers + around
    for peer in partners:
        pl.semaphore_signal(barrier, inc=1, device_id=peer, device_id_type=MESH)

    loads = [
        pltpu.make_async_copy(source, target, in_sem.at[i])
        for i, (source, target) in enumerate(
            [
                (dist_hbm, dist_ref),
                (adjoint_hbm, adjoint_ref),
                (coeffs_hbm, coef.at[:, pad : pad + rows, :]),
                (sources_hbm, src_ref),
            ]
        )
    ]
    for load in loads:
        load.start()
    w_loads = []
    for i in range(W_PARTS):
        part = pl.ds(i * (nblk // W_PARTS), nblk // W_PARTS)
        w_loads.append(pltpu.make_async_copy(weights_hbm.at[part], w_ref.at[part], w_sem.at[i]))
        w_loads[-1].start()

    for load in loads:
        load.wait()
    for c in range(tiles):
        turned[c] = adjoint_ref[:, c * lanes : (c + 1) * lanes]

    @pl.loop(0, rows)
    def _(r):
        keep = 1.0 - davies(dist_ref[pl.ds(r, 1), :])
        for c in range(tiles):
            cut = slice(c * lanes, (c + 1) * lanes)
            field[r + SUB, :, cut] = keep[:, cut] * turned[c, pl.ds(r, levels, stride=rows), :]

    for i in range(4):
        spot = slice(i % 2 * SUB, (i % 2 + 1) * SUB)
        stage[0, i // 2, spot] = coef[i, pad : pad + SUB, :]
        stage[1, i // 2, spot] = coef[i, pad + rows - SUB : pad + rows, :]

    pl.semaphore_wait(barrier, len(partners))

    def halo(at):
        to = {"gy": me - 1 if at == 0 else me + 1}
        first = SUB if at == 0 else rows
        land = rows + SUB if at == 0 else 0
        return [
            pltpu.make_async_remote_copy(
                src_ref=field.at[first : first + SUB],
                dst_ref=field.at[land : land + SUB],
                send_sem=halo_send.at[at, 0],
                recv_sem=halo_recv.at[at, 0],
                device_id=to,
                device_id_type=MESH,
            ),
            pltpu.make_async_remote_copy(
                src_ref=stage.at[at],
                dst_ref=got_stage.at[at],
                send_sem=halo_send.at[at, 1],
                recv_sem=halo_recv.at[at, 1],
                device_id=to,
                device_id_type=MESH,
            ),
        ]

    up, down = halo(0), halo(1)

    @pl.when(me > 0)
    def _():
        for copy in up:
            copy.start()

    @pl.when(me < n - 1)
    def _():
        for copy in down:
            copy.start()

    lane = lax.broadcasted_iota(jnp.int32, (levels, lanes), 1)
    for q in range(rows // per):
        tile = jnp.zeros((levels, lanes), jnp.float32)
        for i in range(per):
            r = q * per + i
            z_left = davies(dist_ref[r : r + 1, :lanes]) * turned[0, pl.ds(r, levels, stride=rows), :]
            z_right = davies(dist_ref[r : r + 1, width - lanes :]) * turned[tiles - 1, pl.ds(r, levels, stride=rows), :]
            both = jnp.where(lane < lanes // 2, z_left, z_right)
            both = pltpu.roll(both, (ZW + 2 * ZW * i) % lanes, 1)
            tile = jnp.where((lane >= 2 * ZW * i) & (lane < 2 * ZW * (i + 1)), both, tile)
        table[q] = tile

    for part in range(W_PARTS):
        w_loads[part].wait()

        @pl.loop(part * (nblk // W_PARTS // STEP_BLOCKS), (part + 1) * (nblk // W_PARTS // STEP_BLOCKS))
        def _(step):
            base = pl.multiple_of(step * STEP_BLOCKS, STEP_BLOCKS)
            src = src_ref[pl.ds(base, STEP_BLOCKS), :]
            row = src // width
            col = src - row * width
            spot = jnp.where(col < ZW, col + ZW, col - (width - ZW)) + (row % per) * (2 * ZW)
            group = row // per
            for j in range(STEP_BLOCKS):
                at = jnp.broadcast_to(spot[j : j + 1, :], (levels, lanes))
                which = jnp.broadcast_to(group[j : j + 1, :], (levels, lanes))
                value = jnp.take_along_axis(table[0], at, axis=1)
                for q in range(1, rows // per):
                    value = jnp.where(which == q, jnp.take_along_axis(table[q], at, axis=1), value)
                out = jnp.dot(value.astype(jnp.bfloat16), w_ref[base + j], preferred_element_type=jnp.float32)
                contrib[pl.ds(base + j, levels, stride=nblk), :] = out

    owner = owner_ref[...]
    own_z, own_x, own_c = owner // (nx * nc), (owner // nc) % nx, owner % nc
    target = ((own_c * nx + own_x) * nz + own_z) * HOST_BLK + slot_ref[...]
    live = lax.broadcasted_iota(jnp.int32, (1, nblk), 1) < count_ref[0]
    target = jnp.where(live, target, -1)
    hosts = n * HOST_BLK
    hit = lax.broadcasted_iota(jnp.int32, (hosts, nblk), 0) == target
    place = jnp.where(hit, 1.0, 0.0).astype(jnp.bfloat16)

    cuts = chunks_of(levels)
    count = len(cuts)
    part_of = lambda i: pl.ds(*cuts[i])
    core_sent, x_sent, z_sent = [], [], []

    def to_core(i):
        for l in range(cuts[i][0], sum(cuts[i])):
            full = split_dot(place, contrib[l * nblk : (l + 1) * nblk, :])
            dense[l] = full.reshape(nc, nx, nz, HOST_BLK, lanes)
        core_sent.append(
            pltpu.make_async_remote_copy(
                src_ref=dense.at[part_of(i), 1 - my_c],
                dst_ref=got_core.at[part_of(i)],
                send_sem=core_send.at[i],
                recv_sem=core_recv.at[i],
                device_id=core_peer,
                device_id_type=MESH,
            )
        )
        core_sent[i].start()

    def along_x(i):
        core_sent[i].wait()
        half[part_of(i), 1 - my_x] = dense[part_of(i), my_c, 1 - my_x] + got_core[part_of(i), 1 - my_x]
        x_sent.append(
            pltpu.make_async_remote_copy(
                src_ref=half.at[part_of(i), 1 - my_x],
                dst_ref=got_x.at[part_of(i)],
                send_sem=x_send.at[i],
                recv_sem=x_recv.at[i],
                device_id=x_peer,
                device_id_type=MESH,
            )
        )
        x_sent[i].start()
        half[part_of(i), my_x] = dense[part_of(i), my_c, my_x] + got_core[part_of(i), my_x]

    for i in range(count):
        to_core(i)
        if i > 0:
            along_x(i - 1)
    along_x(count - 1)

    @pl.when(me == 0)
    def _():
        field[0:SUB] = jnp.zeros((SUB, levels, width), jnp.float32)
        got_stage[1] = jnp.zeros(got_stage.shape[1:], jnp.float32)

    @pl.when(me == n - 1)
    def _():
        field[rows + SUB :] = jnp.zeros((SUB, levels, width), jnp.float32)
        got_stage[0] = jnp.zeros(got_stage.shape[1:], jnp.float32)

    @pl.when(me > 0)
    def _():
        for copy in up:
            copy.wait_send()
        for copy in down:
            copy.wait_recv()

    @pl.when(me < n - 1)
    def _():
        for copy in down:
            copy.wait_send()
        for copy in up:
            copy.wait_recv()

    for i in range(4):
        spot = slice(i % 2 * SUB, (i % 2 + 1) * SUB)
        coef[i, pad - SUB : pad, :] = got_stage[1, i // 2, spot]
        coef[i, pad + rows : pad + rows + SUB, :] = got_stage[0, i // 2, spot]

    column = lax.broadcasted_iota(jnp.int32, (levels, width), 1)

    def k_row(which, r):
        return jnp.broadcast_to(coef[which, pl.ds(r + pad - SUB, 1), :], (levels, width))

    def sweep(step, low, high, carry):

        def body(r, carry):
            from_above, here = carry
            below = field[r + 1]
            k_n, k_s, k_w, k_e = (k_row(i, r) for i in range(4))
            g_west = pltpu.roll(k_w * here, width - 1, 1)
            g_east = pltpu.roll(k_e * here, 1, 1)
            g_west = jnp.where(column == width - 1, 0.0, g_west)
            g_east = jnp.where(column == 0, 0.0, g_east)
            new = here * (1.0 - (k_n + k_s + k_w + k_e)) + k_row(0, r + 1) * below
            new = new + from_above + g_west + g_east
            if step == SUB - 1:
                for c in range(tiles):
                    turned[c, pl.ds(r - SUB, levels, stride=rows), :] = new[:, c * lanes : (c + 1) * lanes]
            else:
                field[r] = new
            return (k_s * here, below)

        if carry is None:
            carry = (k_row(1, low - 1) * field[low - 1], field[low])
        return lax.fori_loop(low, high, body, carry)

    def along_z(i):
        x_sent[i].wait()
        quarter[part_of(i)] = half[part_of(i), my_x] + got_x[part_of(i)]
        for k in range(1, nz):
            z_sent.append(
                pltpu.make_async_remote_copy(
                    src_ref=quarter.at[part_of(i), lax.rem(my_z + k, nz)],
                    dst_ref=got_z.at[k - 1, part_of(i)],
                    send_sem=z_send.at[i, k - 1],
                    recv_sem=z_recv.at[i, k - 1],
                    device_id=z_peers[k - 1],
                    device_id_type=MESH,
                )
            )
            z_sent[-1].start()

    done = 0
    for step in range(SUB):
        low, high = step + 1, rows + 2 * SUB - 1 - step
        carry = sweep(step, low, (low + high) // 2, None)
        if 2 * step + 1 in Z_AFTER:
            along_z(done)
            done += 1
        sweep(step, (low + high) // 2, high, carry)
        if 2 * step + 2 in Z_AFTER:
            along_z(done)
            done += 1
    grads = [
        pltpu.make_async_copy(turned.at[c], grad_ref.at[:, c * lanes : (c + 1) * lanes], out_sem.at[c])
        for c in range(tiles)
    ]
    for copy in grads:
        copy.start()
    for i in range(done, count):
        along_z(i)
    for i in range(count):
        for copy in z_sent[i * (nz - 1) : (i + 1) * (nz - 1)]:
            copy.wait()
        for l in range(cuts[i][0], sum(cuts[i])):
            total = quarter[l, my_z]
            for k in range(nz - 1):
                total = total + got_z[k, l]
            host_ref[pl.ds(l, HOST_BLK, stride=levels), :] = total
    for copy in grads:
        copy.wait()


def fused(n, sizes, adjoint, coeffs, dist, sources, weights, owners, slots, counts):
    levels, rows, width = adjoint.shape
    nblk, block = sources.shape
    lanes = weights.shape[2]
    nz, nx, nc = sizes
    count = len(chunks_of(levels))
    f32 = lambda *shape: pltpu.VMEM(shape, jnp.float32)
    dma = lambda *shape: pltpu.SemaphoreType.DMA(shape)
    hbm = pl.BlockSpec(memory_space=pltpu.HBM)
    vmem = pl.BlockSpec(memory_space=pltpu.VMEM)
    grad, host = pl.pallas_call(
        functools.partial(fused_kernel, n, sizes),
        out_shape=[
            jax.ShapeDtypeStruct((levels * rows, width), jnp.float32),
            jax.ShapeDtypeStruct((HOST_BLK * levels, lanes), jnp.float32),
        ],
        in_specs=[hbm] * 5 + [vmem] * 2 + [pl.BlockSpec(memory_space=pltpu.SMEM)],
        out_specs=[hbm, vmem],
        scratch_shapes=[
            f32(levels * rows, width),
            pltpu.VMEM((rows, width), jnp.int32),
            pltpu.VMEM((nblk, block), jnp.int32),
            pltpu.VMEM((nblk, block, lanes), jnp.bfloat16),
            f32(rows * 2 * ZW // lanes, levels, lanes),
            f32(levels * nblk, lanes),
            f32(rows + 2 * SUB, levels, width),
            f32(4, rows + 16, width),
            f32(2, 2, 2 * SUB, width),
            f32(2, 2, 2 * SUB, width),
            f32(width // lanes, levels * rows, lanes),
            f32(levels, nc, nx, nz, HOST_BLK, lanes),
            f32(levels, nx, nz, HOST_BLK, lanes),
            f32(levels, nx, nz, HOST_BLK, lanes),
            f32(levels, nz, HOST_BLK, lanes),
            f32(levels, nz, HOST_BLK, lanes),
            f32(nz - 1, levels, HOST_BLK, lanes),
            dma(4),
            dma(W_PARTS),
            dma(width // lanes),
            dma(2, 2),
            dma(2, 2),
            dma(count),
            dma(count),
            dma(count),
            dma(count),
            dma(count, nz - 1),
            dma(count, nz - 1),
        ],
        compiler_params=pltpu.CompilerParams(
            collective_id=0, has_side_effects=True, vmem_limit_bytes=62 * 2**20
        ),
        name="fused",
    )(
        adjoint.reshape(levels * rows, width), coeffs, dist, sources, weights,
        owners.reshape(1, nblk), slots.reshape(1, nblk), counts,
    )
    grad = grad.reshape(levels, rows, width)
    host = host.reshape(HOST_BLK, levels, lanes)
    return pl.pallas_call(
        deliver_kernel,
        out_shape=[
            jax.ShapeDtypeStruct(grad.shape, jnp.float32),
            jax.ShapeDtypeStruct(host.shape, jnp.float32),
        ],
        in_specs=[hbm, hbm],
        out_specs=[hbm, hbm],
        scratch_shapes=[dma(2)],
        compiler_params=pltpu.CompilerParams(vmem_limit_bytes=62 * 2**20),
        name="deliver",
    )(grad, host)


def local(adjoint, coeffs, dist, sources, weights, owners, slots, counts):
    levels, rows, width = adjoint.shape
    nblk = sources.shape[0]
    host_width = weights.shape[2]
    owner_count = lax.axis_size("gy")
    capacity = max(2, (2 * nblk + owner_count - 1) // owner_count)
    if owner_count == 16:
        return fused(owner_count, (4, 2, 2), adjoint, coeffs, dist, sources, weights, owners, slots, counts)
    relax = davies(dist)
    k_north, k_south, k_west, k_east = (coeffs[0], coeffs[1], coeffs[2], coeffs[3])
    total = k_north + k_south + k_west + k_east
    zone = (relax * adjoint).reshape(levels, rows * width)
    values = jnp.take(zone, sources, axis=1).astype(jnp.bfloat16)
    contrib = jnp.einsum("lbk,bkh->blh", values, weights, preferred_element_type=jnp.float32)
    live = lax.iota(jnp.int32, nblk) < counts[0]
    flat_contrib = jnp.where(live[:, None, None], contrib, 0.0).reshape(nblk, levels * host_width)
    owner_ids = owners[:, 0]
    onehot = (owner_ids[:, None] == lax.iota(jnp.int32, owner_count)[None, :]).astype(jnp.int32)
    before = jnp.cumsum(onehot, axis=0) - onehot
    position = jnp.sum(before * onehot, axis=1)
    target = owner_ids * capacity + position
    packed = (
        jnp.zeros((owner_count * capacity, levels * host_width), jnp.float32)
        .at[target]
        .set(flat_contrib)
    )
    block_ids = (
        jnp.full((owner_count * capacity,), -1.0, jnp.float32)
        .at[target]
        .set(jnp.where(live, slots.astype(jnp.float32), -1.0))
    )
    received, got_ids = (
        lax.all_to_all(
            packed.reshape(owner_count, capacity, levels * host_width),
            "gy",
            split_axis=0,
            concat_axis=0,
            tiled=True,
        ),
        lax.all_to_all(
            block_ids.reshape(owner_count, capacity), "gy", split_axis=0, concat_axis=0, tiled=True
        ),
    )
    flat_ids = got_ids.reshape(-1).astype(jnp.int32)
    flat_ids = jnp.where(flat_ids >= 0, flat_ids, HOST_BLK)
    buffer = jnp.zeros((HOST_BLK + 1, levels * host_width), jnp.float32)
    host = buffer.at[flat_ids].add(received.reshape(owner_count * capacity, levels * host_width))[
        :HOST_BLK
    ]
    host_adjoint = host.reshape(HOST_BLK, levels, host_width)
    field = (1.0 - relax) * adjoint
    for step in range(SUB):
        g_north = k_north * field
        g_south = k_south * field
        below = from_behind(g_north[:, :1, :], "gy", -1)
        above = from_behind(g_south[:, -1:, :], "gy", 1)
        upper = jnp.concatenate([g_north[:, 1:, :], below], 1)
        lower = jnp.concatenate([above, g_south[:, :-1, :]], 1)
        left_part, right_part = sideways(field, k_west, k_east)
        field = field * (1.0 - total) + upper + lower + left_part + right_part
    return (field, host_adjoint)


def solution(mesh):
    placed = (
        P("groups", "gy", None),
        P(None, "gy", None),
        P("gy", None),
        P("gy", None),
        P("gy", None, None),
        P("gy", None),
        P("gy"),
        P("gy"),
    )
    return jax.shard_map(
        local,
        mesh=mesh,
        in_specs=placed,
        out_specs=(P("groups", "gy", None), P("gy", "groups", None)),
        check_vma=False,
    )
```

```python
import functools

import jax
import jax.numpy as jnp
from jax import lax
from jax.experimental import pallas as pl
from jax.experimental.pallas import tpu as pltpu
from jax.sharding import PartitionSpec as P

ZW = 16
SUB = 4
HOST_BLK = 32
STEP_BLOCKS = 16
W_PARTS = 4
Z_AFTER = (3, 6, 8)
MESH = pl.DeviceIdType.MESH


def from_behind(value, axis, steps):
    count = lax.axis_size(axis)
    initial, last = (max(0, -steps), min(count, count - steps))
    return lax.ppermute(value, axis, [(source, source + steps) for source in range(initial, last)])


def davies(dist):
    frac = 1.0 - dist.astype(jnp.float32) / ZW
    return frac * frac


def sideways(field, k_west, k_east):
    g_west = k_west * field
    g_east = k_east * field
    zero_col = jnp.zeros_like(field[:, :, :1])
    left_part = jnp.concatenate([g_west[:, :, 1:], zero_col], 2)
    right_part = jnp.concatenate([zero_col, g_east[:, :, :-1]], 2)
    return (left_part, right_part)


def split_dot(onehot, x):
    hi = x.astype(jnp.bfloat16)
    lo = (x - hi.astype(jnp.float32)).astype(jnp.bfloat16)
    return jnp.dot(onehot, hi, preferred_element_type=jnp.float32) + jnp.dot(
        onehot, lo, preferred_element_type=jnp.float32
    )


def chunks_of(levels):
    sizes = [2] * (levels // 2 - 1) + [1, 1]
    return [(sum(sizes[:i]), size) for i, size in enumerate(sizes)]


def deliver_kernel(grad_in, host_in, grad_ref, host_ref, grad_held, host_held, in_sem, out_sem):
    levels = grad_in.shape[0]
    parts = levels // 2
    trips = [(grad_in.at[pl.ds(2 * i, 2)], grad_held.at[pl.ds(2 * i, 2)], grad_ref.at[pl.ds(2 * i, 2)]) for i in range(parts)]
    trips.append((host_in, host_held, host_ref))
    arriving = [pltpu.make_async_copy(a, b, in_sem.at[i]) for i, (a, b, c) in enumerate(trips)]
    leaving = [pltpu.make_async_copy(b, c, out_sem.at[i]) for i, (a, b, c) in enumerate(trips)]
    for copy in arriving:
        copy.start()
    for i in range(len(trips)):
        arriving[i].wait()
        leaving[i].start()
    for copy in leaving:
        copy.wait()


def fused_kernel(
    n, sizes, adjoint_hbm, coeffs_hbm, dist_hbm, sources_hbm, weights_hbm, owner_ref, slot_ref, count_ref,
    grad_ref, host_ref,
    adjoint_ref, dist_ref, src_ref, w_ref, table, contrib, field, coef, stage, got_stage, turned,
    dense, got_core, half, got_x, quarter, got_z,
    in_sem, w_sem, out_sem, halo_send, halo_recv, core_send, core_recv, x_send, x_recv, z_send, z_recv,
):
    nz, nx, nc = sizes
    me = lax.axis_index("gy")
    my_z, my_x, my_c = me // (nx * nc), (me // nc) % nx, me % nc
    rows, width = dist_ref.shape
    levels = adjoint_ref.shape[0] // rows
    nblk, lanes = src_ref.shape
    tiles = width // lanes
    pad = 8
    per = lanes // (2 * ZW)

    def at_gy(z, x, c):
        return {"gy": (z * nx + x) * nc + c}

    core_peer = at_gy(my_z, my_x, 1 - my_c)
    x_peer = at_gy(my_z, 1 - my_x, my_c)
    z_peers = [at_gy(lax.rem(my_z + k, nz), my_x, my_c) for k in range(1, nz)]

    barrier = pltpu.get_barrier_semaphore()
    around = [{"gy": lax.rem(me + n - 1, n)}, {"gy": lax.rem(me + 1, n)}]
    partners = [core_peer, x_peer] + z_peers + around
    for peer in partners:
        pl.semaphore_signal(barrier, inc=1, device_id=peer, device_id_type=MESH)

    loads = [
        pltpu.make_async_copy(source, target, in_sem.at[i])
        for i, (source, target) in enumerate(
            [
                (dist_hbm, dist_ref),
                (adjoint_hbm, adjoint_ref),
                (coeffs_hbm, coef.at[:, pad : pad + rows, :]),
                (sources_hbm, src_ref),
            ]
        )
    ]
    for load in loads:
        load.start()
    w_loads = []
    for i in range(W_PARTS):
        part = pl.ds(i * (nblk // W_PARTS), nblk // W_PARTS)
        w_loads.append(pltpu.make_async_copy(weights_hbm.at[part], w_ref.at[part], w_sem.at[i]))
        w_loads[-1].start()

    for load in loads:
        load.wait()
    for c in range(tiles):
        turned[c] = adjoint_ref[:, c * lanes : (c + 1) * lanes]

    @pl.loop(0, rows)
    def _(r):
        keep = 1.0 - davies(dist_ref[pl.ds(r, 1), :])
        for c in range(tiles):
            cut = slice(c * lanes, (c + 1) * lanes)
            field[r + SUB, :, cut] = keep[:, cut] * turned[c, pl.ds(r, levels, stride=rows), :]

    for i in range(4):
        spot = slice(i % 2 * SUB, (i % 2 + 1) * SUB)
        stage[0, i // 2, spot] = coef[i, pad : pad + SUB, :]
        stage[1, i // 2, spot] = coef[i, pad + rows - SUB : pad + rows, :]

    pl.semaphore_wait(barrier, len(partners))

    def halo(at):
        to = {"gy": me - 1 if at == 0 else me + 1}
        first = SUB if at == 0 else rows
        land = rows + SUB if at == 0 else 0
        return [
            pltpu.make_async_remote_copy(
                src_ref=field.at[first : first + SUB],
                dst_ref=field.at[land : land + SUB],
                send_sem=halo_send.at[at, 0],
                recv_sem=halo_recv.at[at, 0],
                device_id=to,
                device_id_type=MESH,
            ),
            pltpu.make_async_remote_copy(
                src_ref=stage.at[at],
                dst_ref=got_stage.at[at],
                send_sem=halo_send.at[at, 1],
                recv_sem=halo_recv.at[at, 1],
                device_id=to,
                device_id_type=MESH,
            ),
        ]

    up, down = halo(0), halo(1)

    @pl.when(me > 0)
    def _():
        for copy in up:
            copy.start()

    @pl.when(me < n - 1)
    def _():
        for copy in down:
            copy.start()

    lane = lax.broadcasted_iota(jnp.int32, (levels, lanes), 1)
    for q in range(rows // per):
        tile = jnp.zeros((levels, lanes), jnp.float32)
        for i in range(per):
            r = q * per + i
            z_left = davies(dist_ref[r : r + 1, :lanes]) * turned[0, pl.ds(r, levels, stride=rows), :]
            z_right = davies(dist_ref[r : r + 1, width - lanes :]) * turned[tiles - 1, pl.ds(r, levels, stride=rows), :]
            both = jnp.where(lane < lanes // 2, z_left, z_right)
            both = pltpu.roll(both, (ZW + 2 * ZW * i) % lanes, 1)
            tile = jnp.where((lane >= 2 * ZW * i) & (lane < 2 * ZW * (i + 1)), both, tile)
        table[q] = tile

    for part in range(W_PARTS):
        w_loads[part].wait()

        @pl.loop(part * (nblk // W_PARTS // STEP_BLOCKS), (part + 1) * (nblk // W_PARTS // STEP_BLOCKS))
        def _(step):
            base = pl.multiple_of(step * STEP_BLOCKS, STEP_BLOCKS)
            src = src_ref[pl.ds(base, STEP_BLOCKS), :]
            row = src // width
            col = src - row * width
            spot = jnp.where(col < ZW, col + ZW, col - (width - ZW)) + (row % per) * (2 * ZW)
            group = row // per
            for j in range(STEP_BLOCKS):
                at = jnp.broadcast_to(spot[j : j + 1, :], (levels, lanes))
                which = jnp.broadcast_to(group[j : j + 1, :], (levels, lanes))
                value = jnp.take_along_axis(table[0], at, axis=1)
                for q in range(1, rows // per):
                    value = jnp.where(which == q, jnp.take_along_axis(table[q], at, axis=1), value)
                out = jnp.dot(value.astype(jnp.bfloat16), w_ref[base + j], preferred_element_type=jnp.float32)
                contrib[pl.ds(base + j, levels, stride=nblk), :] = out

    owner = owner_ref[...]
    own_z, own_x, own_c = owner // (nx * nc), (owner // nc) % nx, owner % nc
    target = ((own_c * nx + own_x) * nz + own_z) * HOST_BLK + slot_ref[...]
    live = lax.broadcasted_iota(jnp.int32, (1, nblk), 1) < count_ref[0]
    target = jnp.where(live, target, -1)
    hosts = n * HOST_BLK
    hit = lax.broadcasted_iota(jnp.int32, (hosts, nblk), 0) == target
    place = jnp.where(hit, 1.0, 0.0).astype(jnp.bfloat16)

    cuts = chunks_of(levels)
    count = len(cuts)
    part_of = lambda i: pl.ds(*cuts[i])
    core_sent, x_sent, z_sent = [], [], []

    def to_core(i):
        for l in range(cuts[i][0], sum(cuts[i])):
            full = split_dot(place, contrib[l * nblk : (l + 1) * nblk, :])
            dense[l] = full.reshape(nc, nx, nz, HOST_BLK, lanes)
        core_sent.append(
            pltpu.make_async_remote_copy(
                src_ref=dense.at[part_of(i), 1 - my_c],
                dst_ref=got_core.at[part_of(i)],
                send_sem=core_send.at[i],
                recv_sem=core_recv.at[i],
                device_id=core_peer,
                device_id_type=MESH,
            )
        )
        core_sent[i].start()

    def along_x(i):
        core_sent[i].wait()
        half[part_of(i), 1 - my_x] = dense[part_of(i), my_c, 1 - my_x] + got_core[part_of(i), 1 - my_x]
        x_sent.append(
            pltpu.make_async_remote_copy(
                src_ref=half.at[part_of(i), 1 - my_x],
                dst_ref=got_x.at[part_of(i)],
                send_sem=x_send.at[i],
                recv_sem=x_recv.at[i],
                device_id=x_peer,
                device_id_type=MESH,
            )
        )
        x_sent[i].start()
        half[part_of(i), my_x] = dense[part_of(i), my_c, my_x] + got_core[part_of(i), my_x]

    for i in range(count):
        to_core(i)
        if i > 0:
            along_x(i - 1)
    along_x(count - 1)

    @pl.when(me == 0)
    def _():
        field[0:SUB] = jnp.zeros((SUB, levels, width), jnp.float32)
        got_stage[1] = jnp.zeros(got_stage.shape[1:], jnp.float32)

    @pl.when(me == n - 1)
    def _():
        field[rows + SUB :] = jnp.zeros((SUB, levels, width), jnp.float32)
        got_stage[0] = jnp.zeros(got_stage.shape[1:], jnp.float32)

    @pl.when(me > 0)
    def _():
        for copy in up:
            copy.wait_send()
        for copy in down:
            copy.wait_recv()

    @pl.when(me < n - 1)
    def _():
        for copy in down:
            copy.wait_send()
        for copy in up:
            copy.wait_recv()

    for i in range(4):
        spot = slice(i % 2 * SUB, (i % 2 + 1) * SUB)
        coef[i, pad - SUB : pad, :] = got_stage[1, i // 2, spot]
        coef[i, pad + rows : pad + rows + SUB, :] = got_stage[0, i // 2, spot]

    column = lax.broadcasted_iota(jnp.int32, (levels, width), 1)

    def k_row(which, r):
        return jnp.broadcast_to(coef[which, pl.ds(r + pad - SUB, 1), :], (levels, width))

    def sweep(step, low, high, carry):

        def body(r, carry):
            from_above, here = carry
            below = field[r + 1]
            k_n, k_s, k_w, k_e = (k_row(i, r) for i in range(4))
            g_west = pltpu.roll(k_w * here, width - 1, 1)
            g_east = pltpu.roll(k_e * here, 1, 1)
            g_west = jnp.where(column == width - 1, 0.0, g_west)
            g_east = jnp.where(column == 0, 0.0, g_east)
            new = here * (1.0 - (k_n + k_s + k_w + k_e)) + k_row(0, r + 1) * below
            new = new + from_above + g_west + g_east
            if step == SUB - 1:
                for c in range(tiles):
                    turned[c, pl.ds(r - SUB, levels, stride=rows), :] = new[:, c * lanes : (c + 1) * lanes]
            else:
                field[r] = new
            return (k_s * here, below)

        if carry is None:
            carry = (k_row(1, low - 1) * field[low - 1], field[low])
        return lax.fori_loop(low, high, body, carry)

    def along_z(i):
        x_sent[i].wait()
        quarter[part_of(i)] = half[part_of(i), my_x] + got_x[part_of(i)]
        for k in range(1, nz):
            z_sent.append(
                pltpu.make_async_remote_copy(
                    src_ref=quarter.at[part_of(i), lax.rem(my_z + k, nz)],
                    dst_ref=got_z.at[k - 1, part_of(i)],
                    send_sem=z_send.at[i, k - 1],
                    recv_sem=z_recv.at[i, k - 1],
                    device_id=z_peers[k - 1],
                    device_id_type=MESH,
                )
            )
            z_sent[-1].start()

    done = 0
    for step in range(SUB):
        low, high = step + 1, rows + 2 * SUB - 1 - step
        carry = sweep(step, low, (low + high) // 2, None)
        if 2 * step + 1 in Z_AFTER:
            along_z(done)
            done += 1
        sweep(step, (low + high) // 2, high, carry)
        if 2 * step + 2 in Z_AFTER:
            along_z(done)
            done += 1
    grads = [
        pltpu.make_async_copy(turned.at[c], grad_ref.at[:, c * lanes : (c + 1) * lanes], out_sem.at[c])
        for c in range(tiles)
    ]
    for copy in grads:
        copy.start()
    for i in range(done, count):
        along_z(i)
    for i in range(count):
        for copy in z_sent[i * (nz - 1) : (i + 1) * (nz - 1)]:
            copy.wait()
        for l in range(cuts[i][0], sum(cuts[i])):
            total = quarter[l, my_z]
            for k in range(nz - 1):
                total = total + got_z[k, l]
            host_ref[pl.ds(l, HOST_BLK, stride=levels), :] = total
    for copy in grads:
        copy.wait()


def fused(n, sizes, adjoint, coeffs, dist, sources, weights, owners, slots, counts):
    levels, rows, width = adjoint.shape
    nblk, block = sources.shape
    lanes = weights.shape[2]
    nz, nx, nc = sizes
    count = len(chunks_of(levels))
    f32 = lambda *shape: pltpu.VMEM(shape, jnp.float32)
    dma = lambda *shape: pltpu.SemaphoreType.DMA(shape)
    hbm = pl.BlockSpec(memory_space=pltpu.HBM)
    vmem = pl.BlockSpec(memory_space=pltpu.VMEM)
    grad, host = pl.pallas_call(
        functools.partial(fused_kernel, n, sizes),
        out_shape=[
            jax.ShapeDtypeStruct((levels * rows, width), jnp.float32),
            jax.ShapeDtypeStruct((HOST_BLK * levels, lanes), jnp.float32),
        ],
        in_specs=[hbm] * 5 + [vmem] * 2 + [pl.BlockSpec(memory_space=pltpu.SMEM)],
        out_specs=[hbm, vmem],
        scratch_shapes=[
            f32(levels * rows, width),
            pltpu.VMEM((rows, width), jnp.int32),
            pltpu.VMEM((nblk, block), jnp.int32),
            pltpu.VMEM((nblk, block, lanes), jnp.bfloat16),
            f32(rows * 2 * ZW // lanes, levels, lanes),
            f32(levels * nblk, lanes),
            f32(rows + 2 * SUB, levels, width),
            f32(4, rows + 16, width),
            f32(2, 2, 2 * SUB, width),
            f32(2, 2, 2 * SUB, width),
            f32(width // lanes, levels * rows, lanes),
            f32(levels, nc, nx, nz, HOST_BLK, lanes),
            f32(levels, nx, nz, HOST_BLK, lanes),
            f32(levels, nx, nz, HOST_BLK, lanes),
            f32(levels, nz, HOST_BLK, lanes),
            f32(levels, nz, HOST_BLK, lanes),
            f32(nz - 1, levels, HOST_BLK, lanes),
            dma(4),
            dma(W_PARTS),
            dma(width // lanes),
            dma(2, 2),
            dma(2, 2),
            dma(count),
            dma(count),
            dma(count),
            dma(count),
            dma(count, nz - 1),
            dma(count, nz - 1),
        ],
        compiler_params=pltpu.CompilerParams(
            collective_id=0, has_side_effects=True, vmem_limit_bytes=62 * 2**20
        ),
        name="fused",
    )(
        adjoint.reshape(levels * rows, width), coeffs, dist, sources, weights,
        owners.reshape(1, nblk), slots.reshape(1, nblk), counts,
    )
    grad = grad.reshape(levels, rows, width)
    host = host.reshape(HOST_BLK, levels, lanes)
    return pl.pallas_call(
        deliver_kernel,
        out_shape=[
            jax.ShapeDtypeStruct(grad.shape, jnp.float32),
            jax.ShapeDtypeStruct(host.shape, jnp.float32),
        ],
        in_specs=[hbm, hbm],
        out_specs=[hbm, hbm],
        scratch_shapes=[f32(*grad.shape), f32(*host.shape), dma(levels // 2 + 1), dma(levels // 2 + 1)],
        compiler_params=pltpu.CompilerParams(vmem_limit_bytes=62 * 2**20),
        name="deliver",
    )(grad, host)


def local(adjoint, coeffs, dist, sources, weights, owners, slots, counts):
    levels, rows, width = adjoint.shape
    nblk = sources.shape[0]
    host_width = weights.shape[2]
    owner_count = lax.axis_size("gy")
    capacity = max(2, (2 * nblk + owner_count - 1) // owner_count)
    if owner_count == 16:
        return fused(owner_count, (4, 2, 2), adjoint, coeffs, dist, sources, weights, owners, slots, counts)
    relax = davies(dist)
    k_north, k_south, k_west, k_east = (coeffs[0], coeffs[1], coeffs[2], coeffs[3])
    total = k_north + k_south + k_west + k_east
    zone = (relax * adjoint).reshape(levels, rows * width)
    values = jnp.take(zone, sources, axis=1).astype(jnp.bfloat16)
    contrib = jnp.einsum("lbk,bkh->blh", values, weights, preferred_element_type=jnp.float32)
    live = lax.iota(jnp.int32, nblk) < counts[0]
    flat_contrib = jnp.where(live[:, None, None], contrib, 0.0).reshape(nblk, levels * host_width)
    owner_ids = owners[:, 0]
    onehot = (owner_ids[:, None] == lax.iota(jnp.int32, owner_count)[None, :]).astype(jnp.int32)
    before = jnp.cumsum(onehot, axis=0) - onehot
    position = jnp.sum(before * onehot, axis=1)
    target = owner_ids * capacity + position
    packed = (
        jnp.zeros((owner_count * capacity, levels * host_width), jnp.float32)
        .at[target]
        .set(flat_contrib)
    )
    block_ids = (
        jnp.full((owner_count * capacity,), -1.0, jnp.float32)
        .at[target]
        .set(jnp.where(live, slots.astype(jnp.float32), -1.0))
    )
    received, got_ids = (
        lax.all_to_all(
            packed.reshape(owner_count, capacity, levels * host_width),
            "gy",
            split_axis=0,
            concat_axis=0,
            tiled=True,
        ),
        lax.all_to_all(
            block_ids.reshape(owner_count, capacity), "gy", split_axis=0, concat_axis=0, tiled=True
        ),
    )
    flat_ids = got_ids.reshape(-1).astype(jnp.int32)
    flat_ids = jnp.where(flat_ids >= 0, flat_ids, HOST_BLK)
    buffer = jnp.zeros((HOST_BLK + 1, levels * host_width), jnp.float32)
    host = buffer.at[flat_ids].add(received.reshape(owner_count * capacity, levels * host_width))[
        :HOST_BLK
    ]
    host_adjoint = host.reshape(HOST_BLK, levels, host_width)
    field = (1.0 - relax) * adjoint
    for step in range(SUB):
        g_north = k_north * field
        g_south = k_south * field
        below = from_behind(g_north[:, :1, :], "gy", -1)
        above = from_behind(g_south[:, -1:, :], "gy", 1)
        upper = jnp.concatenate([g_north[:, 1:, :], below], 1)
        lower = jnp.concatenate([above, g_south[:, :-1, :]], 1)
        left_part, right_part = sideways(field, k_west, k_east)
        field = field * (1.0 - total) + upper + lower + left_part + right_part
    return (field, host_adjoint)


def solution(mesh):
    placed = (
        P("groups", "gy", None),
        P(None, "gy", None),
        P("gy", None),
        P("gy", None),
        P("gy", None, None),
        P("gy", None),
        P("gy"),
        P("gy"),
    )
    return jax.shard_map(
        local,
        mesh=mesh,
        in_specs=placed,
        out_specs=(P("groups", "gy", None), P("gy", "groups", None)),
        check_vma=False,
    )
```

```python
import functools

import jax
import jax.numpy as jnp
from jax import lax
from jax.experimental import pallas as pl
from jax.experimental.pallas import tpu as pltpu
from jax.sharding import PartitionSpec as P

ZW = 16
SUB = 4
HOST_BLK = 32
STEP_BLOCKS = 16
W_PARTS = 4
Z_AFTER = (3, 5, 7, 8)
MESH = pl.DeviceIdType.MESH


def from_behind(value, axis, steps):
    count = lax.axis_size(axis)
    initial, last = (max(0, -steps), min(count, count - steps))
    return lax.ppermute(value, axis, [(source, source + steps) for source in range(initial, last)])


def davies(dist):
    frac = 1.0 - dist.astype(jnp.float32) / ZW
    return frac * frac


def sideways(field, k_west, k_east):
    g_west = k_west * field
    g_east = k_east * field
    zero_col = jnp.zeros_like(field[:, :, :1])
    left_part = jnp.concatenate([g_west[:, :, 1:], zero_col], 2)
    right_part = jnp.concatenate([zero_col, g_east[:, :, :-1]], 2)
    return (left_part, right_part)


def split_dot(onehot, x):
    hi = x.astype(jnp.bfloat16)
    lo = (x - hi.astype(jnp.float32)).astype(jnp.bfloat16)
    return jnp.dot(onehot, hi, preferred_element_type=jnp.float32) + jnp.dot(
        onehot, lo, preferred_element_type=jnp.float32
    )


def chunks_of(levels):
    return [(level, 1) for level in range(levels)]


def deliver_kernel(grad_in, host_in, grad_ref, host_ref, grad_held, host_held, in_sem, out_sem):
    levels = grad_in.shape[0]
    parts = levels // 2
    trips = [(grad_in.at[pl.ds(2 * i, 2)], grad_held.at[pl.ds(2 * i, 2)], grad_ref.at[pl.ds(2 * i, 2)]) for i in range(parts)]
    trips.append((host_in, host_held, host_ref))
    arriving = [pltpu.make_async_copy(a, b, in_sem.at[i]) for i, (a, b, c) in enumerate(trips)]
    leaving = [pltpu.make_async_copy(b, c, out_sem.at[i]) for i, (a, b, c) in enumerate(trips)]
    for copy in arriving:
        copy.start()
    for i in range(len(trips)):
        arriving[i].wait()
        leaving[i].start()
    for copy in leaving:
        copy.wait()


def fused_kernel(
    n, sizes, adjoint_hbm, coeffs_hbm, dist_hbm, sources_hbm, weights_hbm, owner_ref, slot_ref, count_ref,
    grad_ref, host_ref,
    adjoint_ref, dist_ref, src_ref, w_ref, table, contrib, field, coef, stage, got_stage, turned,
    dense, got_core, half, got_x, quarter, got_z,
    in_sem, w_sem, out_sem, halo_send, halo_recv, core_send, core_recv, x_send, x_recv, z_send, z_recv,
):
    nz, nx, nc = sizes
    me = lax.axis_index("gy")
    my_z, my_x, my_c = me // (nx * nc), (me // nc) % nx, me % nc
    rows, width = dist_ref.shape
    levels = adjoint_ref.shape[0] // rows
    nblk, lanes = src_ref.shape
    tiles = width // lanes
    pad = 8
    per = lanes // (2 * ZW)

    def at_gy(z, x, c):
        return {"gy": (z * nx + x) * nc + c}

    core_peer = at_gy(my_z, my_x, 1 - my_c)
    x_peer = at_gy(my_z, 1 - my_x, my_c)
    z_peers = [at_gy(lax.rem(my_z + k, nz), my_x, my_c) for k in range(1, nz)]

    barrier = pltpu.get_barrier_semaphore()
    around = [{"gy": lax.rem(me + n - 1, n)}, {"gy": lax.rem(me + 1, n)}]
    partners = [core_peer, x_peer] + z_peers + around
    for peer in partners:
        pl.semaphore_signal(barrier, inc=1, device_id=peer, device_id_type=MESH)

    loads = [
        pltpu.make_async_copy(source, target, in_sem.at[i])
        for i, (source, target) in enumerate(
            [
                (dist_hbm, dist_ref),
                (adjoint_hbm, adjoint_ref),
                (coeffs_hbm, coef.at[:, pad : pad + rows, :]),
                (sources_hbm, src_ref),
            ]
        )
    ]
    for load in loads:
        load.start()
    w_loads = []
    for i in range(W_PARTS):
        part = pl.ds(i * (nblk // W_PARTS), nblk // W_PARTS)
        w_loads.append(pltpu.make_async_copy(weights_hbm.at[part], w_ref.at[part], w_sem.at[i]))
        w_loads[-1].start()

    for load in loads:
        load.wait()
    for c in range(tiles):
        turned[c] = adjoint_ref[:, c * lanes : (c + 1) * lanes]

    @pl.loop(0, rows)
    def _(r):
        keep = 1.0 - davies(dist_ref[pl.ds(r, 1), :])
        for c in range(tiles):
            cut = slice(c * lanes, (c + 1) * lanes)
            field[r + SUB, :, cut] = keep[:, cut] * turned[c, pl.ds(r, levels, stride=rows), :]

    for i in range(4):
        spot = slice(i % 2 * SUB, (i % 2 + 1) * SUB)
        stage[0, i // 2, spot] = coef[i, pad : pad + SUB, :]
        stage[1, i // 2, spot] = coef[i, pad + rows - SUB : pad + rows, :]

    pl.semaphore_wait(barrier, len(partners))

    def halo(at):
        to = {"gy": me - 1 if at == 0 else me + 1}
        first = SUB if at == 0 else rows
        land = rows + SUB if at == 0 else 0
        return [
            pltpu.make_async_remote_copy(
                src_ref=field.at[first : first + SUB],
                dst_ref=field.at[land : land + SUB],
                send_sem=halo_send.at[at, 0],
                recv_sem=halo_recv.at[at, 0],
                device_id=to,
                device_id_type=MESH,
            ),
            pltpu.make_async_remote_copy(
                src_ref=stage.at[at],
                dst_ref=got_stage.at[at],
                send_sem=halo_send.at[at, 1],
                recv_sem=halo_recv.at[at, 1],
                device_id=to,
                device_id_type=MESH,
            ),
        ]

    up, down = halo(0), halo(1)

    @pl.when(me > 0)
    def _():
        for copy in up:
            copy.start()

    @pl.when(me < n - 1)
    def _():
        for copy in down:
            copy.start()

    lane = lax.broadcasted_iota(jnp.int32, (levels, lanes), 1)
    for q in range(rows // per):
        tile = jnp.zeros((levels, lanes), jnp.float32)
        for i in range(per):
            r = q * per + i
            z_left = davies(dist_ref[r : r + 1, :lanes]) * turned[0, pl.ds(r, levels, stride=rows), :]
            z_right = davies(dist_ref[r : r + 1, width - lanes :]) * turned[tiles - 1, pl.ds(r, levels, stride=rows), :]
            both = jnp.where(lane < lanes // 2, z_left, z_right)
            both = pltpu.roll(both, (ZW + 2 * ZW * i) % lanes, 1)
            tile = jnp.where((lane >= 2 * ZW * i) & (lane < 2 * ZW * (i + 1)), both, tile)
        table[q] = tile

    for part in range(W_PARTS):
        w_loads[part].wait()

        @pl.loop(part * (nblk // W_PARTS // STEP_BLOCKS), (part + 1) * (nblk // W_PARTS // STEP_BLOCKS))
        def _(step):
            base = pl.multiple_of(step * STEP_BLOCKS, STEP_BLOCKS)
            src = src_ref[pl.ds(base, STEP_BLOCKS), :]
            row = src // width
            col = src - row * width
            spot = jnp.where(col < ZW, col + ZW, col - (width - ZW)) + (row % per) * (2 * ZW)
            group = row // per
            for j in range(STEP_BLOCKS):
                at = jnp.broadcast_to(spot[j : j + 1, :], (levels, lanes))
                which = jnp.broadcast_to(group[j : j + 1, :], (levels, lanes))
                value = jnp.take_along_axis(table[0], at, axis=1)
                for q in range(1, rows // per):
                    value = jnp.where(which == q, jnp.take_along_axis(table[q], at, axis=1), value)
                out = jnp.dot(value.astype(jnp.bfloat16), w_ref[base + j], preferred_element_type=jnp.float32)
                contrib[pl.ds(base + j, levels, stride=nblk), :] = out

    owner = owner_ref[...]
    own_z, own_x, own_c = owner // (nx * nc), (owner // nc) % nx, owner % nc
    target = ((own_c * nx + own_x) * nz + own_z) * HOST_BLK + slot_ref[...]
    live = lax.broadcasted_iota(jnp.int32, (1, nblk), 1) < count_ref[0]
    target = jnp.where(live, target, -1)
    hosts = n * HOST_BLK
    hit = lax.broadcasted_iota(jnp.int32, (hosts, nblk), 0) == target
    place = jnp.where(hit, 1.0, 0.0).astype(jnp.bfloat16)

    cuts = chunks_of(levels)
    count = len(cuts)
    part_of = lambda i: pl.ds(*cuts[i])
    core_sent, x_sent, z_sent = [], [], []

    def to_core(i):
        for l in range(cuts[i][0], sum(cuts[i])):
            full = split_dot(place, contrib[l * nblk : (l + 1) * nblk, :])
            dense[l] = full.reshape(nc, nx, nz, HOST_BLK, lanes)
        core_sent.append(
            pltpu.make_async_remote_copy(
                src_ref=dense.at[part_of(i), 1 - my_c],
                dst_ref=got_core.at[part_of(i)],
                send_sem=core_send.at[i],
                recv_sem=core_recv.at[i],
                device_id=core_peer,
                device_id_type=MESH,
            )
        )
        core_sent[i].start()

    def along_x(i):
        core_sent[i].wait()
        half[part_of(i), 1 - my_x] = dense[part_of(i), my_c, 1 - my_x] + got_core[part_of(i), 1 - my_x]
        x_sent.append(
            pltpu.make_async_remote_copy(
                src_ref=half.at[part_of(i), 1 - my_x],
                dst_ref=got_x.at[part_of(i)],
                send_sem=x_send.at[i],
                recv_sem=x_recv.at[i],
                device_id=x_peer,
                device_id_type=MESH,
            )
        )
        x_sent[i].start()
        half[part_of(i), my_x] = dense[part_of(i), my_c, my_x] + got_core[part_of(i), my_x]

    for i in range(count):
        to_core(i)
        if i > 0:
            along_x(i - 1)
    along_x(count - 1)

    @pl.when(me == 0)
    def _():
        field[0:SUB] = jnp.zeros((SUB, levels, width), jnp.float32)
        got_stage[1] = jnp.zeros(got_stage.shape[1:], jnp.float32)

    @pl.when(me == n - 1)
    def _():
        field[rows + SUB :] = jnp.zeros((SUB, levels, width), jnp.float32)
        got_stage[0] = jnp.zeros(got_stage.shape[1:], jnp.float32)

    @pl.when(me > 0)
    def _():
        for copy in up:
            copy.wait_send()
        for copy in down:
            copy.wait_recv()

    @pl.when(me < n - 1)
    def _():
        for copy in down:
            copy.wait_send()
        for copy in up:
            copy.wait_recv()

    for i in range(4):
        spot = slice(i % 2 * SUB, (i % 2 + 1) * SUB)
        coef[i, pad - SUB : pad, :] = got_stage[1, i // 2, spot]
        coef[i, pad + rows : pad + rows + SUB, :] = got_stage[0, i // 2, spot]

    column = lax.broadcasted_iota(jnp.int32, (levels, width), 1)

    def k_row(which, r):
        return jnp.broadcast_to(coef[which, pl.ds(r + pad - SUB, 1), :], (levels, width))

    def sweep(step, low, high, carry):

        def body(r, carry):
            from_above, here = carry
            below = field[r + 1]
            k_n, k_s, k_w, k_e = (k_row(i, r) for i in range(4))
            g_west = pltpu.roll(k_w * here, width - 1, 1)
            g_east = pltpu.roll(k_e * here, 1, 1)
            g_west = jnp.where(column == width - 1, 0.0, g_west)
            g_east = jnp.where(column == 0, 0.0, g_east)
            new = here * (1.0 - (k_n + k_s + k_w + k_e)) + k_row(0, r + 1) * below
            new = new + from_above + g_west + g_east
            if step == SUB - 1:
                for c in range(tiles):
                    turned[c, pl.ds(r - SUB, levels, stride=rows), :] = new[:, c * lanes : (c + 1) * lanes]
            else:
                field[r] = new
            return (k_s * here, below)

        if carry is None:
            carry = (k_row(1, low - 1) * field[low - 1], field[low])
        return lax.fori_loop(low, high, body, carry)

    def along_z(i):
        x_sent[i].wait()
        quarter[part_of(i)] = half[part_of(i), my_x] + got_x[part_of(i)]
        for k in range(1, nz):
            z_sent.append(
                pltpu.make_async_remote_copy(
                    src_ref=quarter.at[part_of(i), lax.rem(my_z + k, nz)],
                    dst_ref=got_z.at[k - 1, part_of(i)],
                    send_sem=z_send.at[i, k - 1],
                    recv_sem=z_recv.at[i, k - 1],
                    device_id=z_peers[k - 1],
                    device_id_type=MESH,
                )
            )
            z_sent[-1].start()

    done = 0
    for step in range(SUB):
        low, high = step + 1, rows + 2 * SUB - 1 - step
        carry = sweep(step, low, (low + high) // 2, None)
        if 2 * step + 1 in Z_AFTER:
            along_z(done)
            done += 1
        sweep(step, (low + high) // 2, high, carry)
        if 2 * step + 2 in Z_AFTER:
            along_z(done)
            done += 1
    grads = [
        pltpu.make_async_copy(turned.at[c], grad_ref.at[:, c * lanes : (c + 1) * lanes], out_sem.at[c])
        for c in range(tiles)
    ]
    for copy in grads:
        copy.start()
    for i in range(done, count):
        along_z(i)
    for i in range(count):
        for copy in z_sent[i * (nz - 1) : (i + 1) * (nz - 1)]:
            copy.wait()
        for l in range(cuts[i][0], sum(cuts[i])):
            total = quarter[l, my_z]
            for k in range(nz - 1):
                total = total + got_z[k, l]
            host_ref[pl.ds(l, HOST_BLK, stride=levels), :] = total
    for copy in grads:
        copy.wait()


def fused(n, sizes, adjoint, coeffs, dist, sources, weights, owners, slots, counts):
    levels, rows, width = adjoint.shape
    nblk, block = sources.shape
    lanes = weights.shape[2]
    nz, nx, nc = sizes
    count = len(chunks_of(levels))
    f32 = lambda *shape: pltpu.VMEM(shape, jnp.float32)
    dma = lambda *shape: pltpu.SemaphoreType.DMA(shape)
    hbm = pl.BlockSpec(memory_space=pltpu.HBM)
    vmem = pl.BlockSpec(memory_space=pltpu.VMEM)
    grad, host = pl.pallas_call(
        functools.partial(fused_kernel, n, sizes),
        out_shape=[
            jax.ShapeDtypeStruct((levels * rows, width), jnp.float32),
            jax.ShapeDtypeStruct((HOST_BLK * levels, lanes), jnp.float32),
        ],
        in_specs=[hbm] * 5 + [vmem] * 2 + [pl.BlockSpec(memory_space=pltpu.SMEM)],
        out_specs=[hbm, vmem],
        scratch_shapes=[
            f32(levels * rows, width),
            pltpu.VMEM((rows, width), jnp.int32),
            pltpu.VMEM((nblk, block), jnp.int32),
            pltpu.VMEM((nblk, block, lanes), jnp.bfloat16),
            f32(rows * 2 * ZW // lanes, levels, lanes),
            f32(levels * nblk, lanes),
            f32(rows + 2 * SUB, levels, width),
            f32(4, rows + 16, width),
            f32(2, 2, 2 * SUB, width),
            f32(2, 2, 2 * SUB, width),
            f32(width // lanes, levels * rows, lanes),
            f32(levels, nc, nx, nz, HOST_BLK, lanes),
            f32(levels, nx, nz, HOST_BLK, lanes),
            f32(levels, nx, nz, HOST_BLK, lanes),
            f32(levels, nz, HOST_BLK, lanes),
            f32(levels, nz, HOST_BLK, lanes),
            f32(nz - 1, levels, HOST_BLK, lanes),
            dma(4),
            dma(W_PARTS),
            dma(width // lanes),
            dma(2, 2),
            dma(2, 2),
            dma(count),
            dma(count),
            dma(count),
            dma(count),
            dma(count, nz - 1),
            dma(count, nz - 1),
        ],
        compiler_params=pltpu.CompilerParams(
            collective_id=0, has_side_effects=True, vmem_limit_bytes=62 * 2**20
        ),
        name="fused",
    )(
        adjoint.reshape(levels * rows, width), coeffs, dist, sources, weights,
        owners.reshape(1, nblk), slots.reshape(1, nblk), counts,
    )
    grad = grad.reshape(levels, rows, width)
    host = host.reshape(HOST_BLK, levels, lanes)
    return pl.pallas_call(
        deliver_kernel,
        out_shape=[
            jax.ShapeDtypeStruct(grad.shape, jnp.float32),
            jax.ShapeDtypeStruct(host.shape, jnp.float32),
        ],
        in_specs=[hbm, hbm],
        out_specs=[hbm, hbm],
        scratch_shapes=[f32(*grad.shape), f32(*host.shape), dma(levels // 2 + 1), dma(levels // 2 + 1)],
        compiler_params=pltpu.CompilerParams(vmem_limit_bytes=62 * 2**20),
        name="deliver",
    )(grad, host)


def local(adjoint, coeffs, dist, sources, weights, owners, slots, counts):
    levels, rows, width = adjoint.shape
    nblk = sources.shape[0]
    host_width = weights.shape[2]
    owner_count = lax.axis_size("gy")
    capacity = max(2, (2 * nblk + owner_count - 1) // owner_count)
    if owner_count == 16:
        return fused(owner_count, (4, 2, 2), adjoint, coeffs, dist, sources, weights, owners, slots, counts)
    relax = davies(dist)
    k_north, k_south, k_west, k_east = (coeffs[0], coeffs[1], coeffs[2], coeffs[3])
    total = k_north + k_south + k_west + k_east
    zone = (relax * adjoint).reshape(levels, rows * width)
    values = jnp.take(zone, sources, axis=1).astype(jnp.bfloat16)
    contrib = jnp.einsum("lbk,bkh->blh", values, weights, preferred_element_type=jnp.float32)
    live = lax.iota(jnp.int32, nblk) < counts[0]
    flat_contrib = jnp.where(live[:, None, None], contrib, 0.0).reshape(nblk, levels * host_width)
    owner_ids = owners[:, 0]
    onehot = (owner_ids[:, None] == lax.iota(jnp.int32, owner_count)[None, :]).astype(jnp.int32)
    before = jnp.cumsum(onehot, axis=0) - onehot
    position = jnp.sum(before * onehot, axis=1)
    target = owner_ids * capacity + position
    packed = (
        jnp.zeros((owner_count * capacity, levels * host_width), jnp.float32)
        .at[target]
        .set(flat_contrib)
    )
    block_ids = (
        jnp.full((owner_count * capacity,), -1.0, jnp.float32)
        .at[target]
        .set(jnp.where(live, slots.astype(jnp.float32), -1.0))
    )
    received, got_ids = (
        lax.all_to_all(
            packed.reshape(owner_count, capacity, levels * host_width),
            "gy",
            split_axis=0,
            concat_axis=0,
            tiled=True,
        ),
        lax.all_to_all(
            block_ids.reshape(owner_count, capacity), "gy", split_axis=0, concat_axis=0, tiled=True
        ),
    )
    flat_ids = got_ids.reshape(-1).astype(jnp.int32)
    flat_ids = jnp.where(flat_ids >= 0, flat_ids, HOST_BLK)
    buffer = jnp.zeros((HOST_BLK + 1, levels * host_width), jnp.float32)
    host = buffer.at[flat_ids].add(received.reshape(owner_count * capacity, levels * host_width))[
        :HOST_BLK
    ]
    host_adjoint = host.reshape(HOST_BLK, levels, host_width)
    field = (1.0 - relax) * adjoint
    for step in range(SUB):
        g_north = k_north * field
        g_south = k_south * field
        below = from_behind(g_north[:, :1, :], "gy", -1)
        above = from_behind(g_south[:, -1:, :], "gy", 1)
        upper = jnp.concatenate([g_north[:, 1:, :], below], 1)
        lower = jnp.concatenate([above, g_south[:, :-1, :]], 1)
        left_part, right_part = sideways(field, k_west, k_east)
        field = field * (1.0 - total) + upper + lower + left_part + right_part
    return (field, host_adjoint)


def solution(mesh):
    placed = (
        P("groups", "gy", None),
        P(None, "gy", None),
        P("gy", None),
        P("gy", None),
        P("gy", None, None),
        P("gy", None),
        P("gy"),
        P("gy"),
    )
    return jax.shard_map(
        local,
        mesh=mesh,
        in_specs=placed,
        out_specs=(P("groups", "gy", None), P("gy", "groups", None)),
        check_vma=False,
    )
```

```python
import functools

import jax
import jax.numpy as jnp
from jax import lax
from jax.experimental import pallas as pl
from jax.experimental.pallas import tpu as pltpu
from jax.sharding import PartitionSpec as P

ZW = 16
SUB = 4
HOST_BLK = 32
STEP_BLOCKS = 16
W_PARTS = 4
Z_AFTER = (3, 5, 7)
MESH = pl.DeviceIdType.MESH


def from_behind(value, axis, steps):
    count = lax.axis_size(axis)
    initial, last = (max(0, -steps), min(count, count - steps))
    return lax.ppermute(value, axis, [(source, source + steps) for source in range(initial, last)])


def davies(dist):
    frac = 1.0 - dist.astype(jnp.float32) / ZW
    return frac * frac


def sideways(field, k_west, k_east):
    g_west = k_west * field
    g_east = k_east * field
    zero_col = jnp.zeros_like(field[:, :, :1])
    left_part = jnp.concatenate([g_west[:, :, 1:], zero_col], 2)
    right_part = jnp.concatenate([zero_col, g_east[:, :, :-1]], 2)
    return (left_part, right_part)


def split_dot(onehot, x):
    hi = x.astype(jnp.bfloat16)
    lo = (x - hi.astype(jnp.float32)).astype(jnp.bfloat16)
    return jnp.dot(onehot, hi, preferred_element_type=jnp.float32) + jnp.dot(
        onehot, lo, preferred_element_type=jnp.float32
    )


def chunks_of(levels):
    sizes = [2,2,2,2]
    return [(sum(sizes[:i]), size) for i, size in enumerate(sizes)]


def deliver_kernel(grad_in, host_in, grad_ref, host_ref, grad_held, host_held, in_sem, out_sem):
    levels = grad_in.shape[0]
    parts = levels // 2
    trips = [(grad_in.at[pl.ds(2 * i, 2)], grad_held.at[pl.ds(2 * i, 2)], grad_ref.at[pl.ds(2 * i, 2)]) for i in range(parts)]
    trips.append((host_in, host_held, host_ref))
    arriving = [pltpu.make_async_copy(a, b, in_sem.at[i]) for i, (a, b, c) in enumerate(trips)]
    leaving = [pltpu.make_async_copy(b, c, out_sem.at[i]) for i, (a, b, c) in enumerate(trips)]
    for copy in arriving:
        copy.start()
    for i in range(len(trips)):
        arriving[i].wait()
        leaving[i].start()
    for copy in leaving:
        copy.wait()


def fused_kernel(
    n, sizes, adjoint_hbm, coeffs_hbm, dist_hbm, sources_hbm, weights_hbm, owner_ref, slot_ref, count_ref,
    grad_ref, host_ref,
    adjoint_ref, dist_ref, src_ref, w_ref, table, contrib, field, coef, stage, got_stage, turned,
    dense, got_core, half, got_x, quarter, got_z,
    in_sem, w_sem, out_sem, halo_send, halo_recv, core_send, core_recv, x_send, x_recv, z_send, z_recv,
):
    nz, nx, nc = sizes
    me = lax.axis_index("gy")
    my_z, my_x, my_c = me // (nx * nc), (me // nc) % nx, me % nc
    rows, width = dist_ref.shape
    levels = adjoint_ref.shape[0] // rows
    nblk, lanes = src_ref.shape
    tiles = width // lanes
    pad = 8
    per = lanes // (2 * ZW)

    def at_gy(z, x, c):
        return {"gy": (z * nx + x) * nc + c}

    core_peer = at_gy(my_z, my_x, 1 - my_c)
    x_peer = at_gy(my_z, 1 - my_x, my_c)
    z_peers = [at_gy(lax.rem(my_z + k, nz), my_x, my_c) for k in range(1, nz)]

    barrier = pltpu.get_barrier_semaphore()
    around = [{"gy": lax.rem(me + n - 1, n)}, {"gy": lax.rem(me + 1, n)}]
    partners = [core_peer, x_peer] + z_peers + around
    for peer in partners:
        pl.semaphore_signal(barrier, inc=1, device_id=peer, device_id_type=MESH)

    loads = [
        pltpu.make_async_copy(source, target, in_sem.at[i])
        for i, (source, target) in enumerate(
            [
                (dist_hbm, dist_ref),
                (adjoint_hbm, adjoint_ref),
                (coeffs_hbm, coef.at[:, pad : pad + rows, :]),
                (sources_hbm, src_ref),
            ]
        )
    ]
    for load in loads:
        load.start()
    w_loads = []
    for i in range(W_PARTS):
        part = pl.ds(i * (nblk // W_PARTS), nblk // W_PARTS)
        w_loads.append(pltpu.make_async_copy(weights_hbm.at[part], w_ref.at[part], w_sem.at[i]))
        w_loads[-1].start()

    for load in loads:
        load.wait()
    for c in range(tiles):
        turned[c] = adjoint_ref[:, c * lanes : (c + 1) * lanes]

    @pl.loop(0, rows)
    def _(r):
        keep = 1.0 - davies(dist_ref[pl.ds(r, 1), :])
        for c in range(tiles):
            cut = slice(c * lanes, (c + 1) * lanes)
            field[r + SUB, :, cut] = keep[:, cut] * turned[c, pl.ds(r, levels, stride=rows), :]

    for i in range(4):
        spot = slice(i % 2 * SUB, (i % 2 + 1) * SUB)
        stage[0, i // 2, spot] = coef[i, pad : pad + SUB, :]
        stage[1, i // 2, spot] = coef[i, pad + rows - SUB : pad + rows, :]

    pl.semaphore_wait(barrier, len(partners))

    def halo(at):
        to = {"gy": me - 1 if at == 0 else me + 1}
        first = SUB if at == 0 else rows
        land = rows + SUB if at == 0 else 0
        return [
            pltpu.make_async_remote_copy(
                src_ref=field.at[first : first + SUB],
                dst_ref=field.at[land : land + SUB],
                send_sem=halo_send.at[at, 0],
                recv_sem=halo_recv.at[at, 0],
                device_id=to,
                device_id_type=MESH,
            ),
            pltpu.make_async_remote_copy(
                src_ref=stage.at[at],
                dst_ref=got_stage.at[at],
                send_sem=halo_send.at[at, 1],
                recv_sem=halo_recv.at[at, 1],
                device_id=to,
                device_id_type=MESH,
            ),
        ]

    up, down = halo(0), halo(1)

    @pl.when(me > 0)
    def _():
        for copy in up:
            copy.start()

    @pl.when(me < n - 1)
    def _():
        for copy in down:
            copy.start()

    lane = lax.broadcasted_iota(jnp.int32, (levels, lanes), 1)
    for q in range(rows // per):
        tile = jnp.zeros((levels, lanes), jnp.float32)
        for i in range(per):
            r = q * per + i
            z_left = davies(dist_ref[r : r + 1, :lanes]) * turned[0, pl.ds(r, levels, stride=rows), :]
            z_right = davies(dist_ref[r : r + 1, width - lanes :]) * turned[tiles - 1, pl.ds(r, levels, stride=rows), :]
            both = jnp.where(lane < lanes // 2, z_left, z_right)
            both = pltpu.roll(both, (ZW + 2 * ZW * i) % lanes, 1)
            tile = jnp.where((lane >= 2 * ZW * i) & (lane < 2 * ZW * (i + 1)), both, tile)
        table[q] = tile

    for part in range(W_PARTS):
        w_loads[part].wait()

        @pl.loop(part * (nblk // W_PARTS // STEP_BLOCKS), (part + 1) * (nblk // W_PARTS // STEP_BLOCKS))
        def _(step):
            base = pl.multiple_of(step * STEP_BLOCKS, STEP_BLOCKS)
            src = src_ref[pl.ds(base, STEP_BLOCKS), :]
            row = src // width
            col = src - row * width
            spot = jnp.where(col < ZW, col + ZW, col - (width - ZW)) + (row % per) * (2 * ZW)
            group = row // per
            for j in range(STEP_BLOCKS):
                at = jnp.broadcast_to(spot[j : j + 1, :], (levels, lanes))
                which = jnp.broadcast_to(group[j : j + 1, :], (levels, lanes))
                value = jnp.take_along_axis(table[0], at, axis=1)
                for q in range(1, rows // per):
                    value = jnp.where(which == q, jnp.take_along_axis(table[q], at, axis=1), value)
                out = jnp.dot(value.astype(jnp.bfloat16), w_ref[base + j], preferred_element_type=jnp.float32)
                contrib[pl.ds(base + j, levels, stride=nblk), :] = out

    owner = owner_ref[...]
    own_z, own_x, own_c = owner // (nx * nc), (owner // nc) % nx, owner % nc
    target = ((own_c * nx + own_x) * nz + own_z) * HOST_BLK + slot_ref[...]
    live = lax.broadcasted_iota(jnp.int32, (1, nblk), 1) < count_ref[0]
    target = jnp.where(live, target, -1)
    hosts = n * HOST_BLK
    hit = lax.broadcasted_iota(jnp.int32, (hosts, nblk), 0) == target
    place = jnp.where(hit, 1.0, 0.0).astype(jnp.bfloat16)

    cuts = chunks_of(levels)
    count = len(cuts)
    part_of = lambda i: pl.ds(*cuts[i])
    core_sent, x_sent, z_sent = [], [], []

    def to_core(i):
        for l in range(cuts[i][0], sum(cuts[i])):
            full = split_dot(place, contrib[l * nblk : (l + 1) * nblk, :])
            dense[l] = full.reshape(nc, nx, nz, HOST_BLK, lanes)
        core_sent.append(
            pltpu.make_async_remote_copy(
                src_ref=dense.at[part_of(i), 1 - my_c],
                dst_ref=got_core.at[part_of(i)],
                send_sem=core_send.at[i],
                recv_sem=core_recv.at[i],
                device_id=core_peer,
                device_id_type=MESH,
            )
        )
        core_sent[i].start()

    def along_x(i):
        core_sent[i].wait()
        half[part_of(i), 1 - my_x] = dense[part_of(i), my_c, 1 - my_x] + got_core[part_of(i), 1 - my_x]
        x_sent.append(
            pltpu.make_async_remote_copy(
                src_ref=half.at[part_of(i), 1 - my_x],
                dst_ref=got_x.at[part_of(i)],
                send_sem=x_send.at[i],
                recv_sem=x_recv.at[i],
                device_id=x_peer,
                device_id_type=MESH,
            )
        )
        x_sent[i].start()
        half[part_of(i), my_x] = dense[part_of(i), my_c, my_x] + got_core[part_of(i), my_x]

    for i in range(count):
        to_core(i)
    for i in range(count):
        along_x(i)

    @pl.when(me == 0)
    def _():
        field[0:SUB] = jnp.zeros((SUB, levels, width), jnp.float32)
        got_stage[1] = jnp.zeros(got_stage.shape[1:], jnp.float32)

    @pl.when(me == n - 1)
    def _():
        field[rows + SUB :] = jnp.zeros((SUB, levels, width), jnp.float32)
        got_stage[0] = jnp.zeros(got_stage.shape[1:], jnp.float32)

    @pl.when(me > 0)
    def _():
        for copy in up:
            copy.wait_send()
        for copy in down:
            copy.wait_recv()

    @pl.when(me < n - 1)
    def _():
        for copy in down:
            copy.wait_send()
        for copy in up:
            copy.wait_recv()

    for i in range(4):
        spot = slice(i % 2 * SUB, (i % 2 + 1) * SUB)
        coef[i, pad - SUB : pad, :] = got_stage[1, i // 2, spot]
        coef[i, pad + rows : pad + rows + SUB, :] = got_stage[0, i // 2, spot]

    column = lax.broadcasted_iota(jnp.int32, (levels, width), 1)

    def k_row(which, r):
        return jnp.broadcast_to(coef[which, pl.ds(r + pad - SUB, 1), :], (levels, width))

    def sweep(step, low, high, carry):

        def body(r, carry):
            from_above, here = carry
            below = field[r + 1]
            k_n, k_s, k_w, k_e = (k_row(i, r) for i in range(4))
            g_west = pltpu.roll(k_w * here, width - 1, 1)
            g_east = pltpu.roll(k_e * here, 1, 1)
            g_west = jnp.where(column == width - 1, 0.0, g_west)
            g_east = jnp.where(column == 0, 0.0, g_east)
            new = here * (1.0 - (k_n + k_s + k_w + k_e)) + k_row(0, r + 1) * below
            new = new + from_above + g_west + g_east
            if step == SUB - 1:
                for c in range(tiles):
                    turned[c, pl.ds(r - SUB, levels, stride=rows), :] = new[:, c * lanes : (c + 1) * lanes]
            else:
                field[r] = new
            return (k_s * here, below)

        if carry is None:
            carry = (k_row(1, low - 1) * field[low - 1], field[low])
        return lax.fori_loop(low, high, body, carry)

    def along_z(i):
        x_sent[i].wait()
        quarter[part_of(i)] = half[part_of(i), my_x] + got_x[part_of(i)]
        for k in range(1, nz):
            z_sent.append(
                pltpu.make_async_remote_copy(
                    src_ref=quarter.at[part_of(i), lax.rem(my_z + k, nz)],
                    dst_ref=got_z.at[k - 1, part_of(i)],
                    send_sem=z_send.at[i, k - 1],
                    recv_sem=z_recv.at[i, k - 1],
                    device_id=z_peers[k - 1],
                    device_id_type=MESH,
                )
            )
            z_sent[-1].start()

    done = 0
    for step in range(SUB):
        low, high = step + 1, rows + 2 * SUB - 1 - step
        carry = sweep(step, low, (low + high) // 2, None)
        if 2 * step + 1 in Z_AFTER:
            along_z(done)
            done += 1
        sweep(step, (low + high) // 2, high, carry)
        if 2 * step + 2 in Z_AFTER:
            along_z(done)
            done += 1
    grads = [
        pltpu.make_async_copy(turned.at[c], grad_ref.at[:, c * lanes : (c + 1) * lanes], out_sem.at[c])
        for c in range(tiles)
    ]
    for copy in grads:
        copy.start()
    for i in range(done, count):
        along_z(i)
    for i in range(count):
        for copy in z_sent[i * (nz - 1) : (i + 1) * (nz - 1)]:
            copy.wait()
        for l in range(cuts[i][0], sum(cuts[i])):
            total = quarter[l, my_z]
            for k in range(nz - 1):
                total = total + got_z[k, l]
            host_ref[pl.ds(l, HOST_BLK, stride=levels), :] = total
    for copy in grads:
        copy.wait()


def fused(n, sizes, adjoint, coeffs, dist, sources, weights, owners, slots, counts):
    levels, rows, width = adjoint.shape
    nblk, block = sources.shape
    lanes = weights.shape[2]
    nz, nx, nc = sizes
    count = len(chunks_of(levels))
    f32 = lambda *shape: pltpu.VMEM(shape, jnp.float32)
    dma = lambda *shape: pltpu.SemaphoreType.DMA(shape)
    hbm = pl.BlockSpec(memory_space=pltpu.HBM)
    vmem = pl.BlockSpec(memory_space=pltpu.VMEM)
    grad, host = pl.pallas_call(
        functools.partial(fused_kernel, n, sizes),
        out_shape=[
            jax.ShapeDtypeStruct((levels * rows, width), jnp.float32),
            jax.ShapeDtypeStruct((HOST_BLK * levels, lanes), jnp.float32),
        ],
        in_specs=[hbm] * 5 + [vmem] * 2 + [pl.BlockSpec(memory_space=pltpu.SMEM)],
        out_specs=[hbm, vmem],
        scratch_shapes=[
            f32(levels * rows, width),
            pltpu.VMEM((rows, width), jnp.int32),
            pltpu.VMEM((nblk, block), jnp.int32),
            pltpu.VMEM((nblk, block, lanes), jnp.bfloat16),
            f32(rows * 2 * ZW // lanes, levels, lanes),
            f32(levels * nblk, lanes),
            f32(rows + 2 * SUB, levels, width),
            f32(4, rows + 16, width),
            f32(2, 2, 2 * SUB, width),
            f32(2, 2, 2 * SUB, width),
            f32(width // lanes, levels * rows, lanes),
            f32(levels, nc, nx, nz, HOST_BLK, lanes),
            f32(levels, nx, nz, HOST_BLK, lanes),
            f32(levels, nx, nz, HOST_BLK, lanes),
            f32(levels, nz, HOST_BLK, lanes),
            f32(levels, nz, HOST_BLK, lanes),
            f32(nz - 1, levels, HOST_BLK, lanes),
            dma(4),
            dma(W_PARTS),
            dma(width // lanes),
            dma(2, 2),
            dma(2, 2),
            dma(count),
            dma(count),
            dma(count),
            dma(count),
            dma(count, nz - 1),
            dma(count, nz - 1),
        ],
        compiler_params=pltpu.CompilerParams(
            collective_id=0, has_side_effects=True, vmem_limit_bytes=62 * 2**20
        ),
        name="fused",
    )(
        adjoint.reshape(levels * rows, width), coeffs, dist, sources, weights,
        owners.reshape(1, nblk), slots.reshape(1, nblk), counts,
    )
    grad = grad.reshape(levels, rows, width)
    host = host.reshape(HOST_BLK, levels, lanes)
    return pl.pallas_call(
        deliver_kernel,
        out_shape=[
            jax.ShapeDtypeStruct(grad.shape, jnp.float32),
            jax.ShapeDtypeStruct(host.shape, jnp.float32),
        ],
        in_specs=[hbm, hbm],
        out_specs=[hbm, hbm],
        scratch_shapes=[f32(*grad.shape), f32(*host.shape), dma(levels // 2 + 1), dma(levels // 2 + 1)],
        compiler_params=pltpu.CompilerParams(vmem_limit_bytes=62 * 2**20),
        name="deliver",
    )(grad, host)


def local(adjoint, coeffs, dist, sources, weights, owners, slots, counts):
    levels, rows, width = adjoint.shape
    nblk = sources.shape[0]
    host_width = weights.shape[2]
    owner_count = lax.axis_size("gy")
    capacity = max(2, (2 * nblk + owner_count - 1) // owner_count)
    if owner_count == 16:
        return fused(owner_count, (4, 2, 2), adjoint, coeffs, dist, sources, weights, owners, slots, counts)
    relax = davies(dist)
    k_north, k_south, k_west, k_east = (coeffs[0], coeffs[1], coeffs[2], coeffs[3])
    total = k_north + k_south + k_west + k_east
    zone = (relax * adjoint).reshape(levels, rows * width)
    values = jnp.take(zone, sources, axis=1).astype(jnp.bfloat16)
    contrib = jnp.einsum("lbk,bkh->blh", values, weights, preferred_element_type=jnp.float32)
    live = lax.iota(jnp.int32, nblk) < counts[0]
    flat_contrib = jnp.where(live[:, None, None], contrib, 0.0).reshape(nblk, levels * host_width)
    owner_ids = owners[:, 0]
    onehot = (owner_ids[:, None] == lax.iota(jnp.int32, owner_count)[None, :]).astype(jnp.int32)
    before = jnp.cumsum(onehot, axis=0) - onehot
    position = jnp.sum(before * onehot, axis=1)
    target = owner_ids * capacity + position
    packed = (
        jnp.zeros((owner_count * capacity, levels * host_width), jnp.float32)
        .at[target]
        .set(flat_contrib)
    )
    block_ids = (
        jnp.full((owner_count * capacity,), -1.0, jnp.float32)
        .at[target]
        .set(jnp.where(live, slots.astype(jnp.float32), -1.0))
    )
    received, got_ids = (
        lax.all_to_all(
            packed.reshape(owner_count, capacity, levels * host_width),
            "gy",
            split_axis=0,
            concat_axis=0,
            tiled=True,
        ),
        lax.all_to_all(
            block_ids.reshape(owner_count, capacity), "gy", split_axis=0, concat_axis=0, tiled=True
        ),
    )
    flat_ids = got_ids.reshape(-1).astype(jnp.int32)
    flat_ids = jnp.where(flat_ids >= 0, flat_ids, HOST_BLK)
    buffer = jnp.zeros((HOST_BLK + 1, levels * host_width), jnp.float32)
    host = buffer.at[flat_ids].add(received.reshape(owner_count * capacity, levels * host_width))[
        :HOST_BLK
    ]
    host_adjoint = host.reshape(HOST_BLK, levels, host_width)
    field = (1.0 - relax) * adjoint
    for step in range(SUB):
        g_north = k_north * field
        g_south = k_south * field
        below = from_behind(g_north[:, :1, :], "gy", -1)
        above = from_behind(g_south[:, -1:, :], "gy", 1)
        upper = jnp.concatenate([g_north[:, 1:, :], below], 1)
        lower = jnp.concatenate([above, g_south[:, :-1, :]], 1)
        left_part, right_part = sideways(field, k_west, k_east)
        field = field * (1.0 - total) + upper + lower + left_part + right_part
    return (field, host_adjoint)


def solution(mesh):
    placed = (
        P("groups", "gy", None),
        P(None, "gy", None),
        P("gy", None),
        P("gy", None),
        P("gy", None, None),
        P("gy", None),
        P("gy"),
        P("gy"),
    )
    return jax.shard_map(
        local,
        mesh=mesh,
        in_specs=placed,
        out_specs=(P("groups", "gy", None), P("gy", "groups", None)),
        check_vma=False,
    )
```

```python
import functools

import jax
import jax.numpy as jnp
from jax import lax
from jax.experimental import pallas as pl
from jax.experimental.pallas import tpu as pltpu
from jax.sharding import PartitionSpec as P

ZW = 16
SUB = 4
HOST_BLK = 32
STEP_BLOCKS = 16
W_PARTS = 4
Z_AFTER = (3, 5, 7)
MESH = pl.DeviceIdType.MESH


def from_behind(value, axis, steps):
    count = lax.axis_size(axis)
    initial, last = (max(0, -steps), min(count, count - steps))
    return lax.ppermute(value, axis, [(source, source + steps) for source in range(initial, last)])


def davies(dist):
    frac = 1.0 - dist.astype(jnp.float32) / ZW
    return frac * frac


def sideways(field, k_west, k_east):
    g_west = k_west * field
    g_east = k_east * field
    zero_col = jnp.zeros_like(field[:, :, :1])
    left_part = jnp.concatenate([g_west[:, :, 1:], zero_col], 2)
    right_part = jnp.concatenate([zero_col, g_east[:, :, :-1]], 2)
    return (left_part, right_part)


def split_dot(onehot, x):
    hi = x.astype(jnp.bfloat16)
    lo = (x - hi.astype(jnp.float32)).astype(jnp.bfloat16)
    return jnp.dot(onehot, hi, preferred_element_type=jnp.float32) + jnp.dot(
        onehot, lo, preferred_element_type=jnp.float32
    )


def chunks_of(levels):
    sizes = [2,2,2,2]
    return [(sum(sizes[:i]), size) for i, size in enumerate(sizes)]


def deliver_kernel(grad_in, host_in, grad_ref, host_ref, grad_held, host_held, in_sem, out_sem):
    levels = grad_in.shape[0]
    parts = levels // 2
    trips = [(grad_in.at[pl.ds(2 * i, 2)], grad_held.at[pl.ds(2 * i, 2)], grad_ref.at[pl.ds(2 * i, 2)]) for i in range(parts)]
    trips.append((host_in, host_held, host_ref))
    arriving = [pltpu.make_async_copy(a, b, in_sem.at[i]) for i, (a, b, c) in enumerate(trips)]
    leaving = [pltpu.make_async_copy(b, c, out_sem.at[i]) for i, (a, b, c) in enumerate(trips)]
    for copy in arriving:
        copy.start()
    for i in range(len(trips)):
        arriving[i].wait()
        leaving[i].start()
    for copy in leaving:
        copy.wait()


def fused_kernel(
    n, sizes, adjoint_hbm, coeffs_hbm, dist_hbm, sources_hbm, weights_hbm, owner_ref, slot_ref, count_ref,
    grad_ref, host_ref,
    adjoint_ref, dist_ref, src_ref, w_ref, table, contrib, field, coef, stage, got_stage, turned,
    dense, got_core, half, got_x, quarter, got_z,
    in_sem, w_sem, out_sem, halo_send, halo_recv, core_send, core_recv, x_send, x_recv, z_send, z_recv,
):
    nz, nx, nc = sizes
    me = lax.axis_index("gy")
    my_z, my_x, my_c = me // (nx * nc), (me // nc) % nx, me % nc
    rows, width = dist_ref.shape
    levels = adjoint_ref.shape[0] // rows
    nblk, lanes = src_ref.shape
    tiles = width // lanes
    pad = 8
    per = lanes // (2 * ZW)

    def at_gy(z, x, c):
        return {"gy": (z * nx + x) * nc + c}

    core_peer = at_gy(my_z, my_x, 1 - my_c)
    x_peer = at_gy(my_z, 1 - my_x, my_c)
    z_peers = [at_gy(lax.rem(my_z + k, nz), my_x, my_c) for k in range(1, nz)]

    barrier = pltpu.get_barrier_semaphore()
    around = [{"gy": lax.rem(me + n - 1, n)}, {"gy": lax.rem(me + 1, n)}]
    partners = [core_peer, x_peer] + z_peers + around
    for peer in partners:
        pl.semaphore_signal(barrier, inc=1, device_id=peer, device_id_type=MESH)

    loads = [
        pltpu.make_async_copy(source, target, in_sem.at[i])
        for i, (source, target) in enumerate(
            [
                (dist_hbm, dist_ref),
                (adjoint_hbm, adjoint_ref),
                (coeffs_hbm, coef.at[:, pad : pad + rows, :]),
                (sources_hbm, src_ref),
            ]
        )
    ]
    for load in loads:
        load.start()
    w_loads = []
    for i in range(W_PARTS):
        part = pl.ds(i * (nblk // W_PARTS), nblk // W_PARTS)
        w_loads.append(pltpu.make_async_copy(weights_hbm.at[part], w_ref.at[part], w_sem.at[i]))
        w_loads[-1].start()

    for load in loads:
        load.wait()
    for c in range(tiles):
        turned[c] = adjoint_ref[:, c * lanes : (c + 1) * lanes]

    @pl.loop(0, rows)
    def _(r):
        keep = 1.0 - davies(dist_ref[pl.ds(r, 1), :])
        for c in range(tiles):
            cut = slice(c * lanes, (c + 1) * lanes)
            field[r + SUB, :, cut] = keep[:, cut] * turned[c, pl.ds(r, levels, stride=rows), :]

    for i in range(4):
        spot = slice(i % 2 * SUB, (i % 2 + 1) * SUB)
        stage[0, i // 2, spot] = coef[i, pad : pad + SUB, :]
        stage[1, i // 2, spot] = coef[i, pad + rows - SUB : pad + rows, :]

    pl.semaphore_wait(barrier, len(partners))

    def halo(at):
        to = {"gy": me - 1 if at == 0 else me + 1}
        first = SUB if at == 0 else rows
        land = rows + SUB if at == 0 else 0
        return [
            pltpu.make_async_remote_copy(
                src_ref=field.at[first : first + SUB],
                dst_ref=field.at[land : land + SUB],
                send_sem=halo_send.at[at, 0],
                recv_sem=halo_recv.at[at, 0],
                device_id=to,
                device_id_type=MESH,
            ),
            pltpu.make_async_remote_copy(
                src_ref=stage.at[at],
                dst_ref=got_stage.at[at],
                send_sem=halo_send.at[at, 1],
                recv_sem=halo_recv.at[at, 1],
                device_id=to,
                device_id_type=MESH,
            ),
        ]

    up, down = halo(0), halo(1)

    @pl.when(me > 0)
    def _():
        for copy in up:
            copy.start()

    @pl.when(me < n - 1)
    def _():
        for copy in down:
            copy.start()

    lane = lax.broadcasted_iota(jnp.int32, (levels, lanes), 1)
    for q in range(rows // per):
        tile = jnp.zeros((levels, lanes), jnp.float32)
        for i in range(per):
            r = q * per + i
            z_left = davies(dist_ref[r : r + 1, :lanes]) * turned[0, pl.ds(r, levels, stride=rows), :]
            z_right = davies(dist_ref[r : r + 1, width - lanes :]) * turned[tiles - 1, pl.ds(r, levels, stride=rows), :]
            both = jnp.where(lane < lanes // 2, z_left, z_right)
            both = pltpu.roll(both, (ZW + 2 * ZW * i) % lanes, 1)
            tile = jnp.where((lane >= 2 * ZW * i) & (lane < 2 * ZW * (i + 1)), both, tile)
        table[q] = tile

    for part in range(W_PARTS):
        w_loads[part].wait()

        @pl.loop(part * (nblk // W_PARTS // STEP_BLOCKS), (part + 1) * (nblk // W_PARTS // STEP_BLOCKS))
        def _(step):
            base = pl.multiple_of(step * STEP_BLOCKS, STEP_BLOCKS)
            src = src_ref[pl.ds(base, STEP_BLOCKS), :]
            row = src // width
            col = src - row * width
            spot = jnp.where(col < ZW, col + ZW, col - (width - ZW)) + (row % per) * (2 * ZW)
            group = row // per
            for j in range(STEP_BLOCKS):
                at = jnp.broadcast_to(spot[j : j + 1, :], (levels, lanes))
                which = jnp.broadcast_to(group[j : j + 1, :], (levels, lanes))
                value = jnp.take_along_axis(table[0], at, axis=1)
                for q in range(1, rows // per):
                    value = jnp.where(which == q, jnp.take_along_axis(table[q], at, axis=1), value)
                out = jnp.dot(value.astype(jnp.bfloat16), w_ref[base + j], preferred_element_type=jnp.float32)
                contrib[pl.ds(base + j, levels, stride=nblk), :] = out

    owner = owner_ref[...]
    own_z, own_x, own_c = owner // (nx * nc), (owner // nc) % nx, owner % nc
    target = ((own_c * nx + own_x) * nz + own_z) * HOST_BLK + slot_ref[...]
    live = lax.broadcasted_iota(jnp.int32, (1, nblk), 1) < count_ref[0]
    target = jnp.where(live, target, -1)
    hosts = n * HOST_BLK
    hit = lax.broadcasted_iota(jnp.int32, (hosts, nblk), 0) == target
    place = jnp.where(hit, 1.0, 0.0).astype(jnp.bfloat16)

    cuts = chunks_of(levels)
    count = len(cuts)
    part_of = lambda i: pl.ds(*cuts[i])
    core_sent, x_sent, z_sent = [], [], []

    def to_core(i):
        for l in range(cuts[i][0], sum(cuts[i])):
            full = split_dot(place, contrib[l * nblk : (l + 1) * nblk, :])
            dense[l] = full.reshape(nc, nx, nz, HOST_BLK, lanes)
        core_sent.append(
            pltpu.make_async_remote_copy(
                src_ref=dense.at[part_of(i), 1 - my_c],
                dst_ref=got_core.at[part_of(i)],
                send_sem=core_send.at[i],
                recv_sem=core_recv.at[i],
                device_id=core_peer,
                device_id_type=MESH,
            )
        )
        core_sent[i].start()

    def along_x(i):
        core_sent[i].wait()
        half[part_of(i), 1 - my_x] = dense[part_of(i), my_c, 1 - my_x] + got_core[part_of(i), 1 - my_x]
        x_sent.append(
            pltpu.make_async_remote_copy(
                src_ref=half.at[part_of(i), 1 - my_x],
                dst_ref=got_x.at[part_of(i)],
                send_sem=x_send.at[i],
                recv_sem=x_recv.at[i],
                device_id=x_peer,
                device_id_type=MESH,
            )
        )
        x_sent[i].start()
        half[part_of(i), my_x] = dense[part_of(i), my_c, my_x] + got_core[part_of(i), my_x]

    for i in range(count):
        to_core(i)
    for i in range(count):
        along_x(i)

    @pl.when(me == 0)
    def _():
        field[0:SUB] = jnp.zeros((SUB, levels, width), jnp.float32)
        got_stage[1] = jnp.zeros(got_stage.shape[1:], jnp.float32)

    @pl.when(me == n - 1)
    def _():
        field[rows + SUB :] = jnp.zeros((SUB, levels, width), jnp.float32)
        got_stage[0] = jnp.zeros(got_stage.shape[1:], jnp.float32)

    @pl.when(me > 0)
    def _():
        for copy in up:
            copy.wait_send()
        for copy in down:
            copy.wait_recv()

    @pl.when(me < n - 1)
    def _():
        for copy in down:
            copy.wait_send()
        for copy in up:
            copy.wait_recv()

    for i in range(4):
        spot = slice(i % 2 * SUB, (i % 2 + 1) * SUB)
        coef[i, pad - SUB : pad, :] = got_stage[1, i // 2, spot]
        coef[i, pad + rows : pad + rows + SUB, :] = got_stage[0, i // 2, spot]

    column = lax.broadcasted_iota(jnp.int32, (levels, width), 1)

    def k_row(which, r):
        return jnp.broadcast_to(coef[which, pl.ds(r + pad - SUB, 1), :], (levels, width))

    def sweep(step, low, high, carry):

        def body(r, carry):
            from_above, here = carry
            below = field[r + 1]
            k_n, k_s, k_w, k_e = (k_row(i, r) for i in range(4))
            g_west = pltpu.roll(k_w * here, width - 1, 1)
            g_east = pltpu.roll(k_e * here, 1, 1)
            g_west = jnp.where(column == width - 1, 0.0, g_west)
            g_east = jnp.where(column == 0, 0.0, g_east)
            new = here * (1.0 - (k_n + k_s + k_w + k_e)) + k_row(0, r + 1) * below
            new = new + from_above + g_west + g_east
            if step == SUB - 1:
                for c in range(tiles):
                    turned[c, pl.ds(r - SUB, levels, stride=rows), :] = new[:, c * lanes : (c + 1) * lanes]
            else:
                field[r] = new
            return (k_s * here, below)

        if carry is None:
            carry = (k_row(1, low - 1) * field[low - 1], field[low])
        return lax.fori_loop(low, high, body, carry)

    def along_z(i):
        x_sent[i].wait()
        quarter[part_of(i)] = half[part_of(i), my_x] + got_x[part_of(i)]
        for k in [2, 1, 3]:
            z_sent.append(
                pltpu.make_async_remote_copy(
                    src_ref=quarter.at[part_of(i), lax.rem(my_z + k, nz)],
                    dst_ref=got_z.at[k - 1, part_of(i)],
                    send_sem=z_send.at[i, k - 1],
                    recv_sem=z_recv.at[i, k - 1],
                    device_id=z_peers[k - 1],
                    device_id_type=MESH,
                )
            )
            z_sent[-1].start()

    done = 0
    for step in range(SUB):
        low, high = step + 1, rows + 2 * SUB - 1 - step
        carry = sweep(step, low, (low + high) // 2, None)
        if 2 * step + 1 in Z_AFTER:
            along_z(done)
            done += 1
        sweep(step, (low + high) // 2, high, carry)
        if 2 * step + 2 in Z_AFTER:
            along_z(done)
            done += 1
    grads = [
        pltpu.make_async_copy(turned.at[c], grad_ref.at[:, c * lanes : (c + 1) * lanes], out_sem.at[c])
        for c in range(tiles)
    ]
    for copy in grads:
        copy.start()
    for i in range(done, count):
        along_z(i)
    for i in range(count):
        for copy in z_sent[i * (nz - 1) : (i + 1) * (nz - 1)]:
            copy.wait()
        for l in range(cuts[i][0], sum(cuts[i])):
            total = quarter[l, my_z]
            for k in range(nz - 1):
                total = total + got_z[k, l]
            host_ref[pl.ds(l, HOST_BLK, stride=levels), :] = total
    for copy in grads:
        copy.wait()


def fused(n, sizes, adjoint, coeffs, dist, sources, weights, owners, slots, counts):
    levels, rows, width = adjoint.shape
    nblk, block = sources.shape
    lanes = weights.shape[2]
    nz, nx, nc = sizes
    count = len(chunks_of(levels))
    f32 = lambda *shape: pltpu.VMEM(shape, jnp.float32)
    dma = lambda *shape: pltpu.SemaphoreType.DMA(shape)
    hbm = pl.BlockSpec(memory_space=pltpu.HBM)
    vmem = pl.BlockSpec(memory_space=pltpu.VMEM)
    grad, host = pl.pallas_call(
        functools.partial(fused_kernel, n, sizes),
        out_shape=[
            jax.ShapeDtypeStruct((levels * rows, width), jnp.float32),
            jax.ShapeDtypeStruct((HOST_BLK * levels, lanes), jnp.float32),
        ],
        in_specs=[hbm] * 5 + [vmem] * 2 + [pl.BlockSpec(memory_space=pltpu.SMEM)],
        out_specs=[hbm, vmem],
        scratch_shapes=[
            f32(levels * rows, width),
            pltpu.VMEM((rows, width), jnp.int32),
            pltpu.VMEM((nblk, block), jnp.int32),
            pltpu.VMEM((nblk, block, lanes), jnp.bfloat16),
            f32(rows * 2 * ZW // lanes, levels, lanes),
            f32(levels * nblk, lanes),
            f32(rows + 2 * SUB, levels, width),
            f32(4, rows + 16, width),
            f32(2, 2, 2 * SUB, width),
            f32(2, 2, 2 * SUB, width),
            f32(width // lanes, levels * rows, lanes),
            f32(levels, nc, nx, nz, HOST_BLK, lanes),
            f32(levels, nx, nz, HOST_BLK, lanes),
            f32(levels, nx, nz, HOST_BLK, lanes),
            f32(levels, nz, HOST_BLK, lanes),
            f32(levels, nz, HOST_BLK, lanes),
            f32(nz - 1, levels, HOST_BLK, lanes),
            dma(4),
            dma(W_PARTS),
            dma(width // lanes),
            dma(2, 2),
            dma(2, 2),
            dma(count),
            dma(count),
            dma(count),
            dma(count),
            dma(count, nz - 1),
            dma(count, nz - 1),
        ],
        compiler_params=pltpu.CompilerParams(
            collective_id=0, has_side_effects=True, vmem_limit_bytes=62 * 2**20
        ),
        name="fused",
    )(
        adjoint.reshape(levels * rows, width), coeffs, dist, sources, weights,
        owners.reshape(1, nblk), slots.reshape(1, nblk), counts,
    )
    grad = grad.reshape(levels, rows, width)
    host = host.reshape(HOST_BLK, levels, lanes)
    return pl.pallas_call(
        deliver_kernel,
        out_shape=[
            jax.ShapeDtypeStruct(grad.shape, jnp.float32),
            jax.ShapeDtypeStruct(host.shape, jnp.float32),
        ],
        in_specs=[hbm, hbm],
        out_specs=[hbm, hbm],
        scratch_shapes=[f32(*grad.shape), f32(*host.shape), dma(levels // 2 + 1), dma(levels // 2 + 1)],
        compiler_params=pltpu.CompilerParams(vmem_limit_bytes=62 * 2**20),
        name="deliver",
    )(grad, host)


def local(adjoint, coeffs, dist, sources, weights, owners, slots, counts):
    levels, rows, width = adjoint.shape
    nblk = sources.shape[0]
    host_width = weights.shape[2]
    owner_count = lax.axis_size("gy")
    capacity = max(2, (2 * nblk + owner_count - 1) // owner_count)
    if owner_count == 16:
        return fused(owner_count, (4, 2, 2), adjoint, coeffs, dist, sources, weights, owners, slots, counts)
    relax = davies(dist)
    k_north, k_south, k_west, k_east = (coeffs[0], coeffs[1], coeffs[2], coeffs[3])
    total = k_north + k_south + k_west + k_east
    zone = (relax * adjoint).reshape(levels, rows * width)
    values = jnp.take(zone, sources, axis=1).astype(jnp.bfloat16)
    contrib = jnp.einsum("lbk,bkh->blh", values, weights, preferred_element_type=jnp.float32)
    live = lax.iota(jnp.int32, nblk) < counts[0]
    flat_contrib = jnp.where(live[:, None, None], contrib, 0.0).reshape(nblk, levels * host_width)
    owner_ids = owners[:, 0]
    onehot = (owner_ids[:, None] == lax.iota(jnp.int32, owner_count)[None, :]).astype(jnp.int32)
    before = jnp.cumsum(onehot, axis=0) - onehot
    position = jnp.sum(before * onehot, axis=1)
    target = owner_ids * capacity + position
    packed = (
        jnp.zeros((owner_count * capacity, levels * host_width), jnp.float32)
        .at[target]
        .set(flat_contrib)
    )
    block_ids = (
        jnp.full((owner_count * capacity,), -1.0, jnp.float32)
        .at[target]
        .set(jnp.where(live, slots.astype(jnp.float32), -1.0))
    )
    received, got_ids = (
        lax.all_to_all(
            packed.reshape(owner_count, capacity, levels * host_width),
            "gy",
            split_axis=0,
            concat_axis=0,
            tiled=True,
        ),
        lax.all_to_all(
            block_ids.reshape(owner_count, capacity), "gy", split_axis=0, concat_axis=0, tiled=True
        ),
    )
    flat_ids = got_ids.reshape(-1).astype(jnp.int32)
    flat_ids = jnp.where(flat_ids >= 0, flat_ids, HOST_BLK)
    buffer = jnp.zeros((HOST_BLK + 1, levels * host_width), jnp.float32)
    host = buffer.at[flat_ids].add(received.reshape(owner_count * capacity, levels * host_width))[
        :HOST_BLK
    ]
    host_adjoint = host.reshape(HOST_BLK, levels, host_width)
    field = (1.0 - relax) * adjoint
    for step in range(SUB):
        g_north = k_north * field
        g_south = k_south * field
        below = from_behind(g_north[:, :1, :], "gy", -1)
        above = from_behind(g_south[:, -1:, :], "gy", 1)
        upper = jnp.concatenate([g_north[:, 1:, :], below], 1)
        lower = jnp.concatenate([above, g_south[:, :-1, :]], 1)
        left_part, right_part = sideways(field, k_west, k_east)
        field = field * (1.0 - total) + upper + lower + left_part + right_part
    return (field, host_adjoint)


def solution(mesh):
    placed = (
        P("groups", "gy", None),
        P(None, "gy", None),
        P("gy", None),
        P("gy", None),
        P("gy", None, None),
        P("gy", None),
        P("gy"),
        P("gy"),
    )
    return jax.shard_map(
        local,
        mesh=mesh,
        in_specs=placed,
        out_specs=(P("groups", "gy", None), P("gy", "groups", None)),
        check_vma=False,
    )
```
